256 devices in a mesh: row: 16 (over z, core), col: 16 (over y, x).
Axes of the slice: x: 4, y: 4, z: 8, core: 2. Of those that a mesh axis runs over, the one named last changes fastest.
Arguments:
- momentum: bfloat16 [8192, 26624], P('row', 'col'), may hold values from -6 to 6
- gradient: bfloat16 [8192, 26624], P('row', 'col'), may hold values from -180 to 180
- right_factor: bfloat16 [26624, 512], P('col'), may hold values from -6 to 6
Outputs:
- new_momentum: bfloat16 [8192, 26624], P('row', 'col')
- weight_update: bfloat16 [8192, 26624], P('row', 'col')
- new_factor: float32 [26624, 512], P('col')
The draws below stay inside these ranges and needn't reach their ends.
All inputs are finite; a program needn't handle non-finite values.
Results may differ from the reference program's by a relative error of at most 0.013.
Values may be sent and summed in bfloat16 or wider, within the bound.
No kernel may reach another device: no remote copies, remote signals or barrier semaphores. Data moves between devices by JAX's collectives and lax.ppermute only.
A program may use at most 64 MiB of HBM per device.

```python
import math
import jax
import jax.numpy as jnp
from jax import lax

ROWS = 8192
COLS = 26624
RANK = 512


def draw_gradient(key, part):
    key = jax.random.fold_in(key, 7)
    subkeys = jax.random.split(key, 3)
    row_ramp = jnp.exp(math.log(3.0) * jnp.arange(ROWS, dtype=jnp.float32) / ROWS)
    col_ramp = jnp.exp(math.log(3.0) * jnp.arange(COLS, dtype=jnp.float32) / COLS)
    spread = math.log(10.0)
    noise_values = jax.random.truncated_normal(subkeys[2], -6.0, 6.0, (ROWS, COLS), jnp.float32)
    divisor = 30.0
    row_scale = jnp.exp(spread * jax.random.uniform(subkeys[0], (ROWS,), jnp.float32)) * row_ramp
    col_scale = jnp.exp(spread * jax.random.uniform(subkeys[1], (COLS,), jnp.float32)) * col_ramp
    values = noise_values * row_scale[:, None] * col_scale[None, :] / divisor
    return values.astype(jnp.bfloat16)


def steps_of(stream_key, shape, cuts, smallest, largest):
    factor_of = 1.0
    for position, parts in cuts:
        steps = jax.random.uniform(jax.random.fold_in(jax.random.fold_in(stream_key, 6), position), (parts,), jnp.float32, smallest / len(cuts), largest / len(cuts))
        factor_of = factor_of * jnp.repeat(jnp.exp(steps), shape[position] // parts).reshape((-1,) + (1,) * (len(shape) - 1 - position))
    return factor_of


def normal_values(key, dims, scale, bound, pieces=(), kind=jnp.bfloat16):
    loudness = steps_of(key, dims, pieces, -0.22, 0.18) if pieces else 1.0
    result = jax.random.normal(key, dims, jnp.float32) * scale * loudness
    return jnp.minimum(jnp.maximum(result, -bound), bound).astype(kind)


def setup_inputs(seed: int = 0) -> dict:
    seeds = jax.random.split(jax.random.key(seed), 4)
    return {
        "momentum": normal_values(seeds[0], (ROWS, COLS), 1.0, 6.0, ((0, 16), (1, 16))),
        "gradient": draw_gradient(jax.random.fold_in(seeds[3], 71), 0),
        "right_factor": normal_values(seeds[2], (COLS, RANK), 1.0, 6.0, ((0, 16),)),
    }


NORM_EPS = 1e-06
GRAM_JITTER = 0.0001
FEEDBACK = 0.25

def reference(momentum, gradient, right_factor):
    blended = (momentum.astype(jnp.float32) + gradient.astype(jnp.float32)).astype(jnp.bfloat16)
    projected = jnp.dot(blended.astype(jnp.float32), right_factor.astype(jnp.float32), preferred_element_type=jnp.float32)
    raw = jnp.dot(projected.T.astype(jnp.float32), projected.astype(jnp.float32), precision=lax.Precision.HIGHEST, preferred_element_type=jnp.float32)
    jitter = GRAM_JITTER * jnp.trace(raw) / RANK
    gram_matrix = raw + jitter * jnp.eye(RANK, dtype=jnp.float32)
    lower_factor = jnp.linalg.cholesky(gram_matrix)
    orthonormal = jax.scipy.linalg.solve_triangular(lower_factor, projected.T, lower=True).T
    left_bf = orthonormal.astype(jnp.bfloat16)
    back = lax.dot_general(blended.astype(jnp.float32), left_bf.astype(jnp.float32), (((0,), (0,)), ((), ())), preferred_element_type=jnp.float32)
    right_bf = back.astype(jnp.bfloat16)
    back_squares = lax.optimization_barrier(jnp.sum(back * back, axis=0))
    new_factor = back / jnp.sqrt(back_squares / COLS + NORM_EPS)
    factor_bf = new_factor.astype(jnp.bfloat16)
    correction = lax.dot_general(left_bf.astype(jnp.float32), right_bf.astype(jnp.float32), (((1,), (1,)), ((), ())), preferred_element_type=jnp.float32)
    new_momentum = (blended.astype(jnp.float32) - FEEDBACK * correction).astype(jnp.bfloat16)
    update_full = lax.dot_general(left_bf.astype(jnp.float32), factor_bf.astype(jnp.float32), (((1,), (1,)), ((), ())), preferred_element_type=jnp.float32)
    weight_update = (update_full * math.sqrt(ROWS / RANK)).astype(jnp.bfloat16)
    return (new_momentum, weight_update, new_factor)
```

```python
import math

import jax
import jax.numpy as jnp
from jax import lax
from jax.experimental import pallas as pl
from jax.experimental.pallas import tpu as pltpu
from jax.sharding import PartitionSpec as P

ROWS = 8192
COLS = 26624
RANK = 512


NORM_EPS = 1e-06
GRAM_JITTER = 0.0001
FEEDBACK = 0.25

HIGHEST = lax.Precision.HIGHEST
BLOCK = 128
BLOCKS = RANK // BLOCK
SUB = 8
GROUPS = BLOCK // SUB
PAIRS = [(i, j) for i in range(BLOCKS) for j in range(i, BLOCKS)]


def sub_row(x, k):
    return jnp.broadcast_to(x[k : k + 1, :], (SUB, BLOCK))


def lane_col(x, c):
    return jnp.broadcast_to(x[:, c : c + 1], (SUB, BLOCK))


def inverse_of(d):
    r = pl.reciprocal(d, approx=True)
    r = r * (2.0 - d * r)
    return r * (2.0 - d * r)


def factor_block(rows, inv):
    sub = lax.broadcasted_iota(jnp.int32, (SUB, BLOCK), 0)
    out = []
    for p in range(GROUPS):
        cols = [lane_col(rows[p], SUB * p + j) for j in range(SUB)]
        pivots, recips, row_k, inv_k, upper = [], [], [], [], []
        for k in range(SUB):
            pivot = sub_row(cols[k], k)
            r = inverse_of(pivot)
            m = jnp.where(sub > k, cols[k] * r, 0.0)
            u = {j: sub_row(cols[j], k) for j in range(k + 1, SUB)}
            for j in range(k + 1, SUB):
                cols[j] = cols[j] - m * u[j]
            vk, ek = sub_row(rows[p], k), sub_row(inv[p], k)
            if k < SUB - 1:
                rows[p] = rows[p] - m * vk
                inv[p] = inv[p] - m * ek
            pivots.append(pivot)
            recips.append(r)
            row_k.append(vk)
            inv_k.append(ek)
            upper.append(u)
        d8 = pivots[0]
        for k in range(1, SUB):
            d8 = jnp.where(sub == k, pivots[k], d8)
        out.append(inv[p] * lax.rsqrt(d8))
        for q in range(p + 1, GROUPS):
            b = [lane_col(rows[q], SUB * p + j) for j in range(SUB)]
            for k in range(SUB):
                m = b[k] * recips[k]
                for j in range(k + 1, SUB):
                    b[j] = b[j] - m * upper[k][j]
                rows[q] = rows[q] - m * row_k[k]
                inv[q] = inv[q] - m * inv_k[k]
    return out


def inverse_factor_kernel(g_ref, m_ref, s_ref, d_ref):
    lane = lax.broadcasted_iota(jnp.int32, (SUB, BLOCK), 1)
    sub = lax.broadcasted_iota(jnp.int32, (SUB, BLOCK), 0)
    eye = (
        lax.broadcasted_iota(jnp.int32, (BLOCK, BLOCK), 0)
        == lax.broadcasted_iota(jnp.int32, (BLOCK, BLOCK), 1)
    )
    diagonal = jnp.zeros((BLOCK, BLOCK), jnp.float32)
    for n, (i, j) in enumerate(PAIRS):
        if i == j:
            diagonal += jnp.where(eye, g_ref[n], 0.0)
    jitter = (GRAM_JITTER / RANK) * jnp.sum(diagonal)
    s_ref[...] = jnp.zeros_like(s_ref)
    for n, (i, j) in enumerate(PAIRS):
        x = g_ref[n]
        if i == j:
            x = x + jnp.where(eye, jitter, 0.0)
        s_ref[BLOCK * i : BLOCK * (i + 1), BLOCK * j : BLOCK * (j + 1)] = x

    def block(b, carry):
        lo = pl.multiple_of(b * BLOCK, BLOCK)
        rows = [s_ref[pl.ds(lo + SUB * q, SUB), pl.ds(lo, BLOCK)] for q in range(GROUPS)]
        inv = [jnp.where(lane == sub + SUB * q, 1.0, 0.0) for q in range(GROUPS)]
        for q, x in enumerate(factor_block(rows, inv)):
            d_ref[SUB * q : SUB * (q + 1), :] = x
        m_bb = d_ref[...]
        s_ref[pl.ds(lo, BLOCK), :] = jnp.dot(
            m_bb, s_ref[pl.ds(lo, BLOCK), :], precision=HIGHEST, preferred_element_type=jnp.float32
        )
        s_ref[pl.ds(lo, BLOCK), pl.ds(lo, BLOCK)] = m_bb
        for i in range(1, BLOCKS):

            @pl.when(i > b)
            def _():
                here = slice(BLOCK * i, BLOCK * (i + 1))
                s_ref[here, pl.ds(lo, BLOCK)] = jnp.zeros((BLOCK, BLOCK), jnp.float32)
                s_ref[here, :] -= lax.dot_general(
                    s_ref[pl.ds(lo, BLOCK), here],
                    s_ref[pl.ds(lo, BLOCK), :],
                    (((0,), (0,)), ((), ())),
                    precision=HIGHEST,
                    preferred_element_type=jnp.float32,
                )

        return carry

    lax.fori_loop(0, BLOCKS, block, 0)
    for i in range(BLOCKS):
        for j in range(BLOCKS):
            here = (slice(BLOCK * i, BLOCK * (i + 1)), slice(BLOCK * j, BLOCK * (j + 1)))
            m_ref[here] = s_ref[here] if j <= i else jnp.zeros((BLOCK, BLOCK), jnp.float32)


def inverse_factor(blocks):
    return pl.pallas_call(
        inverse_factor_kernel,
        out_shape=jax.ShapeDtypeStruct((RANK, RANK), jnp.float32),
        in_specs=[pl.BlockSpec(memory_space=pltpu.VMEM)],
        out_specs=pl.BlockSpec(memory_space=pltpu.VMEM),
        scratch_shapes=[pltpu.VMEM((RANK, RANK), jnp.float32), pltpu.VMEM((BLOCK, BLOCK), jnp.float32)],
        compiler_params=pltpu.CompilerParams(vmem_limit_bytes=16 * 1024 * 1024),
        cost_estimate=pl.CostEstimate(flops=2**30, bytes_accessed=2**21, transcendentals=0),
    )(blocks)


def scatter_sum(x, axis, groups, size):
    parts = x.reshape((size, x.shape[0] // size) + x.shape[1:])
    return jnp.sum(lax.all_to_all(parts, axis, 0, 0, axis_index_groups=groups), axis=0)


def gather(x, axis, groups, size):
    parts = jnp.broadcast_to(x, (size,) + x.shape)
    parts = lax.all_to_all(parts, axis, 0, 0, axis_index_groups=groups)
    return parts.reshape((size * x.shape[0],) + x.shape[1:])


def split3(x):
    hi = lax.reduce_precision(x, 8, 7)
    rest = x - hi
    mid = lax.reduce_precision(rest, 8, 7)
    return hi.astype(jnp.bfloat16), mid.astype(jnp.bfloat16), (rest - mid).astype(jnp.bfloat16)


def local(momentum, gradient, right_factor):
    n_col = lax.axis_size("col")
    n_row = lax.axis_size("row")
    n_z = n_row // 2
    core = lax.axis_index("row") % 2
    other = [(i, i ^ 1) for i in range(n_row)]
    along_z = [[2 * z + c for z in range(n_z)] for c in range(2)]

    def my_half(x):
        halves = x.reshape((2, x.shape[0] // 2) + x.shape[1:])
        mine = lax.dynamic_index_in_dim(halves, core, 0, keepdims=False)
        return mine + lax.ppermute(lax.dynamic_index_in_dim(halves, 1 - core, 0, keepdims=False), "row", other)

    def both_halves(mine):
        theirs = lax.ppermute(mine, "row", other)
        return jnp.concatenate([jnp.where(core == 0, mine, theirs), jnp.where(core == 0, theirs, mine)])

    blended = (momentum.astype(jnp.float32) + gradient.astype(jnp.float32)).astype(jnp.bfloat16)
    partial_proj = jnp.dot(blended, right_factor, preferred_element_type=jnp.float32)
    projected = gather(scatter_sum(partial_proj, "col", None, n_col), "col", None, n_col)

    gram = jnp.dot(projected.T, projected, precision=HIGHEST, preferred_element_type=jnp.float32)
    packed = jnp.concatenate(
        [gram[BLOCK * i : BLOCK * (i + 1), BLOCK * j : BLOCK * (j + 1)] for i, j in PAIRS]
    )
    packed = gather(scatter_sum(my_half(packed), "row", along_z, n_z), "row", along_z, n_z)
    packed = both_halves(packed).reshape(len(PAIRS), BLOCK, BLOCK)

    weights = 0.0
    for piece in split3(projected):
        weights += lax.dot_general(
            blended, piece, (((0,), (0,)), ((), ())), preferred_element_type=jnp.float32
        )
    weights = both_halves(lax.psum(my_half(weights), "row", axis_index_groups=along_z))

    inverse = inverse_factor(packed)
    left_bf = jnp.dot(
        projected, inverse.T, precision=HIGHEST, preferred_element_type=jnp.float32
    ).astype(jnp.bfloat16)
    back = jnp.dot(weights, inverse.T, precision=HIGHEST, preferred_element_type=jnp.float32)
    squares = jnp.sum(back * back, axis=0).reshape(BLOCKS, BLOCK)
    squares = lax.all_to_all(jnp.broadcast_to(squares, (n_col, BLOCKS, BLOCK)), "col", 0, 0)
    back_squares = jnp.sum(squares, axis=0).reshape(RANK)
    right_bf = back.astype(jnp.bfloat16)
    new_factor = back / jnp.sqrt(back_squares / COLS + NORM_EPS)
    factor_bf = new_factor.astype(jnp.bfloat16)
    correction = lax.dot_general(
        left_bf, right_bf, (((1,), (1,)), ((), ())), preferred_element_type=jnp.float32
    )
    new_momentum = (blended.astype(jnp.float32) - FEEDBACK * correction).astype(jnp.bfloat16)
    update_full = lax.dot_general(
        left_bf, factor_bf, (((1,), (1,)), ((), ())), preferred_element_type=jnp.float32
    )
    weight_update = (update_full * math.sqrt(ROWS / RANK)).astype(jnp.bfloat16)
    return (new_momentum, weight_update, new_factor)


def solution(mesh):
    placed = (P("row", "col"), P("row", "col"), P("col", None))
    return jax.shard_map(
        local,
        mesh=mesh,
        in_specs=placed,
        out_specs=(P("row", "col"), P("row", "col"), P("col", None)),
        check_vma=False,
    )
```

```python
import math

import jax
import jax.numpy as jnp
from jax import lax
from jax.experimental import pallas as pl
from jax.experimental.pallas import tpu as pltpu
from jax.sharding import PartitionSpec as P

ROWS = 8192
COLS = 26624
RANK = 512


NORM_EPS = 1e-06
GRAM_JITTER = 0.0001
FEEDBACK = 0.25

HIGHEST = lax.Precision.HIGHEST
BLOCK = 128
BLOCKS = RANK // BLOCK
SUB = 8
GROUPS = BLOCK // SUB
PAIRS = [(i, j) for i in range(BLOCKS) for j in range(i, BLOCKS)]


def sub_row(x, k):
    return jnp.broadcast_to(x[k : k + 1, :], (SUB, BLOCK))


def lane_col(x, c):
    return jnp.broadcast_to(x[:, c : c + 1], (SUB, BLOCK))


def inverse_of(d):
    r = pl.reciprocal(d, approx=True)
    r = r * (2.0 - d * r)
    return r * (2.0 - d * r)


def factor_block(rows, inv):
    sub = lax.broadcasted_iota(jnp.int32, (SUB, BLOCK), 0)
    out = []
    for p in range(GROUPS):
        cols = [lane_col(rows[p], SUB * p + j) for j in range(SUB)]
        pivots, recips, row_k, inv_k, upper = [], [], [], [], []
        for k in range(SUB):
            pivot = sub_row(cols[k], k)
            r = inverse_of(pivot)
            m = jnp.where(sub > k, cols[k] * r, 0.0)
            u = {j: sub_row(cols[j], k) for j in range(k + 1, SUB)}
            for j in range(k + 1, SUB):
                cols[j] = cols[j] - m * u[j]
            vk, ek = sub_row(rows[p], k), sub_row(inv[p], k)
            if k < SUB - 1:
                rows[p] = rows[p] - m * vk
                inv[p] = inv[p] - m * ek
            pivots.append(pivot)
            recips.append(r)
            row_k.append(vk)
            inv_k.append(ek)
            upper.append(u)
        d8 = pivots[0]
        for k in range(1, SUB):
            d8 = jnp.where(sub == k, pivots[k], d8)
        out.append(inv[p] * lax.rsqrt(d8))
        for q in range(p + 1, GROUPS):
            b = [lane_col(rows[q], SUB * p + j) for j in range(SUB)]
            for k in range(SUB):
                m = b[k] * recips[k]
                for j in range(k + 1, SUB):
                    b[j] = b[j] - m * upper[k][j]
                rows[q] = rows[q] - m * row_k[k]
                inv[q] = inv[q] - m * inv_k[k]
    return out


def inverse_factor_kernel(g_ref, m_ref, s_ref, d_ref):
    lane = lax.broadcasted_iota(jnp.int32, (SUB, BLOCK), 1)
    sub = lax.broadcasted_iota(jnp.int32, (SUB, BLOCK), 0)
    eye = (
        lax.broadcasted_iota(jnp.int32, (BLOCK, BLOCK), 0)
        == lax.broadcasted_iota(jnp.int32, (BLOCK, BLOCK), 1)
    )
    diagonal = jnp.zeros((BLOCK, BLOCK), jnp.float32)
    for n, (i, j) in enumerate(PAIRS):
        if i == j:
            diagonal += jnp.where(eye, g_ref[n], 0.0)
    jitter = (GRAM_JITTER / RANK) * jnp.sum(diagonal)
    s_ref[...] = jnp.zeros_like(s_ref)
    for n, (i, j) in enumerate(PAIRS):
        x = g_ref[n]
        if i == j:
            x = x + jnp.where(eye, jitter, 0.0)
        s_ref[BLOCK * i : BLOCK * (i + 1), BLOCK * j : BLOCK * (j + 1)] = x

    def block(b, carry):
        lo = pl.multiple_of(b * BLOCK, BLOCK)
        rows = [s_ref[pl.ds(lo + SUB * q, SUB), pl.ds(lo, BLOCK)] for q in range(GROUPS)]
        inv = [jnp.where(lane == sub + SUB * q, 1.0, 0.0) for q in range(GROUPS)]
        for q, x in enumerate(factor_block(rows, inv)):
            d_ref[SUB * q : SUB * (q + 1), :] = x
        m_bb = d_ref[...]
        s_ref[pl.ds(lo, BLOCK), :] = jnp.dot(
            m_bb, s_ref[pl.ds(lo, BLOCK), :], precision=HIGHEST, preferred_element_type=jnp.float32
        )
        s_ref[pl.ds(lo, BLOCK), pl.ds(lo, BLOCK)] = m_bb
        for i in range(1, BLOCKS):

            @pl.when(i > b)
            def _():
                here = slice(BLOCK * i, BLOCK * (i + 1))
                s_ref[here, pl.ds(lo, BLOCK)] = jnp.zeros((BLOCK, BLOCK), jnp.float32)
                s_ref[here, :] -= lax.dot_general(
                    s_ref[pl.ds(lo, BLOCK), here],
                    s_ref[pl.ds(lo, BLOCK), :],
                    (((0,), (0,)), ((), ())),
                    precision=HIGHEST,
                    preferred_element_type=jnp.float32,
                )

        return carry

    lax.fori_loop(0, BLOCKS, block, 0)
    for i in range(BLOCKS):
        for j in range(BLOCKS):
            here = (slice(BLOCK * i, BLOCK * (i + 1)), slice(BLOCK * j, BLOCK * (j + 1)))
            m_ref[here] = s_ref[here] if j <= i else jnp.zeros((BLOCK, BLOCK), jnp.float32)


def gram_kernel(p_ref, o_ref):
    for i in range(BLOCKS):
        rows = lax.dot_general(
            p_ref[:, BLOCK * i : BLOCK * (i + 1)],
            p_ref[:, BLOCK * i :],
            (((0,), (0,)), ((), ())),
            precision=HIGHEST,
            preferred_element_type=jnp.float32,
        )
        for j in range(i, BLOCKS):
            o_ref[PAIRS.index((i, j))] = rows[:, BLOCK * (j - i) : BLOCK * (j - i + 1)]


def gram_blocks(projected):
    return pl.pallas_call(
        gram_kernel,
        out_shape=jax.ShapeDtypeStruct((len(PAIRS), BLOCK, BLOCK), jnp.float32),
        in_specs=[pl.BlockSpec(memory_space=pltpu.VMEM)],
        out_specs=pl.BlockSpec(memory_space=pltpu.VMEM),
        compiler_params=pltpu.CompilerParams(vmem_limit_bytes=16 * 1024 * 1024),
        cost_estimate=pl.CostEstimate(flops=2**31, bytes_accessed=2**21, transcendentals=0),
    )(projected)


def inverse_factor(blocks):
    return pl.pallas_call(
        inverse_factor_kernel,
        out_shape=jax.ShapeDtypeStruct((RANK, RANK), jnp.float32),
        in_specs=[pl.BlockSpec(memory_space=pltpu.VMEM)],
        out_specs=pl.BlockSpec(memory_space=pltpu.VMEM),
        scratch_shapes=[pltpu.VMEM((RANK, RANK), jnp.float32), pltpu.VMEM((BLOCK, BLOCK), jnp.float32)],
        compiler_params=pltpu.CompilerParams(vmem_limit_bytes=16 * 1024 * 1024),
        cost_estimate=pl.CostEstimate(flops=2**34, bytes_accessed=2**21, transcendentals=0),
    )(blocks)


def scatter_sum(x, axis, groups, size):
    parts = x.reshape((size, x.shape[0] // size) + x.shape[1:]) if x.shape[0] != size else x
    return jnp.sum(lax.all_to_all(parts, axis, 0, 0, axis_index_groups=groups), axis=0)


def gather(x, axis, groups, size):
    parts = jnp.broadcast_to(x, (size,) + x.shape)
    parts = lax.all_to_all(parts, axis, 0, 0, axis_index_groups=groups)
    return parts.reshape((size * x.shape[0],) + x.shape[1:])


def split3(x):
    hi = lax.reduce_precision(x, 8, 7)
    rest = x - hi
    mid = lax.reduce_precision(rest, 8, 7)
    return hi.astype(jnp.bfloat16), mid.astype(jnp.bfloat16), (rest - mid).astype(jnp.bfloat16)


def local(momentum, gradient, right_factor):
    n_col = lax.axis_size("col")
    n_row = lax.axis_size("row")
    n_z = n_row // 2
    core = lax.axis_index("row") % 2
    other = [(i, i ^ 1) for i in range(n_row)]
    along_z = [[2 * z + c for z in range(n_z)] for c in range(2)]

    def my_half(x):
        halves = x.reshape((2, x.shape[0] // 2) + x.shape[1:])
        mine = lax.dynamic_index_in_dim(halves, core, 0, keepdims=False)
        return mine + lax.ppermute(lax.dynamic_index_in_dim(halves, 1 - core, 0, keepdims=False), "row", other)

    def both_halves(mine):
        theirs = lax.ppermute(mine, "row", other)
        return jnp.concatenate([jnp.where(core == 0, mine, theirs), jnp.where(core == 0, theirs, mine)])

    blended = (momentum.astype(jnp.float32) + gradient.astype(jnp.float32)).astype(jnp.bfloat16)
    partial_proj = jnp.dot(blended, right_factor, preferred_element_type=jnp.float32)
    projected = gather(scatter_sum(partial_proj, "col", None, n_col), "col", None, n_col)

    packed = gram_blocks(projected).reshape(len(PAIRS) * BLOCK, BLOCK)
    packed, projected = lax.optimization_barrier((my_half(packed), projected))
    packed = gather(scatter_sum(packed, "row", along_z, n_z), "row", along_z, n_z)
    packed = both_halves(packed).reshape(len(PAIRS), BLOCK, BLOCK)

    weights = 0.0
    for piece in split3(projected):
        weights += lax.dot_general(
            blended, piece, (((0,), (0,)), ((), ())), preferred_element_type=jnp.float32
        )
    weights = lax.psum_scatter(
        my_half(weights), "row", scatter_dimension=0, axis_index_groups=along_z, tiled=True
    )

    inverse = inverse_factor(packed)
    back_rows = jnp.dot(weights, inverse.T, precision=HIGHEST, preferred_element_type=jnp.float32)
    right_bf = both_halves(gather(back_rows.astype(jnp.bfloat16), "row", along_z, n_z))
    squares = jnp.sum(back_rows * back_rows, axis=0).reshape(BLOCKS, BLOCK)
    squares = scatter_sum(jnp.broadcast_to(squares, (n_col, BLOCKS, BLOCK)), "col", None, n_col)
    squares = scatter_sum(jnp.broadcast_to(squares, (n_row, BLOCKS, BLOCK)), "row", None, n_row)
    back_squares = squares.reshape(RANK)
    left_bf = jnp.dot(
        projected, inverse.T, precision=HIGHEST, preferred_element_type=jnp.float32
    ).astype(jnp.bfloat16)
    new_factor = right_bf.astype(jnp.float32) / jnp.sqrt(back_squares / COLS + NORM_EPS)
    factor_bf = new_factor.astype(jnp.bfloat16)
    correction = lax.dot_general(
        left_bf, right_bf, (((1,), (1,)), ((), ())), preferred_element_type=jnp.float32
    )
    new_momentum = (blended.astype(jnp.float32) - FEEDBACK * correction).astype(jnp.bfloat16)
    update_full = lax.dot_general(
        left_bf, factor_bf, (((1,), (1,)), ((), ())), preferred_element_type=jnp.float32
    )
    weight_update = (update_full * math.sqrt(ROWS / RANK)).astype(jnp.bfloat16)
    return (new_momentum, weight_update, new_factor)


def solution(mesh):
    placed = (P("row", "col"), P("row", "col"), P("col", None))
    return jax.shard_map(
        local,
        mesh=mesh,
        in_specs=placed,
        out_specs=(P("row", "col"), P("row", "col"), P("col", None)),
        check_vma=False,
    )
```

```python
import math

import jax
import jax.numpy as jnp
from jax import lax
from jax.experimental import pallas as pl
from jax.experimental.pallas import tpu as pltpu
from jax.sharding import PartitionSpec as P

ROWS = 8192
COLS = 26624
RANK = 512


NORM_EPS = 1e-06
GRAM_JITTER = 0.0001
FEEDBACK = 0.25

HIGHEST = lax.Precision.HIGHEST
BLOCK = 128
BLOCKS = RANK // BLOCK
SUB = 8
GROUPS = BLOCK // SUB
PAIRS = [(i, j) for i in range(BLOCKS) for j in range(i, BLOCKS)]


def sub_row(x, k):
    return jnp.broadcast_to(x[k : k + 1, :], (SUB, BLOCK))


def lane_col(x, c):
    return jnp.broadcast_to(x[:, c : c + 1], (SUB, BLOCK))


def inverse_of(d):
    r = pl.reciprocal(d, approx=True)
    r = r * (2.0 - d * r)
    return r * (2.0 - d * r)


def factor_block(rows, inv):
    sub = lax.broadcasted_iota(jnp.int32, (SUB, BLOCK), 0)
    out = []
    for p in range(GROUPS):
        cols = [lane_col(rows[p], SUB * p + j) for j in range(SUB)]
        pivots, recips, row_k, inv_k, upper = [], [], [], [], []
        for k in range(SUB):
            pivot = sub_row(cols[k], k)
            r = inverse_of(pivot)
            m = jnp.where(sub > k, cols[k] * r, 0.0)
            u = {j: sub_row(cols[j], k) for j in range(k + 1, SUB)}
            for j in range(k + 1, SUB):
                cols[j] = cols[j] - m * u[j]
            vk, ek = sub_row(rows[p], k), sub_row(inv[p], k)
            if k < SUB - 1:
                rows[p] = rows[p] - m * vk
                inv[p] = inv[p] - m * ek
            pivots.append(pivot)
            recips.append(r)
            row_k.append(vk)
            inv_k.append(ek)
            upper.append(u)
        d8 = pivots[0]
        for k in range(1, SUB):
            d8 = jnp.where(sub == k, pivots[k], d8)
        out.append(inv[p] * lax.rsqrt(d8))
        for q in range(p + 1, GROUPS):
            b = [lane_col(rows[q], SUB * p + j) for j in range(SUB)]
            for k in range(SUB):
                m = b[k] * recips[k]
                for j in range(k + 1, SUB):
                    b[j] = b[j] - m * upper[k][j]
                rows[q] = rows[q] - m * row_k[k]
                inv[q] = inv[q] - m * inv_k[k]
    return out


def inverse_factor_kernel(g_ref, m_ref, s_ref, d_ref):
    lane = lax.broadcasted_iota(jnp.int32, (SUB, BLOCK), 1)
    sub = lax.broadcasted_iota(jnp.int32, (SUB, BLOCK), 0)
    eye = (
        lax.broadcasted_iota(jnp.int32, (BLOCK, BLOCK), 0)
        == lax.broadcasted_iota(jnp.int32, (BLOCK, BLOCK), 1)
    )
    diagonal = jnp.zeros((BLOCK, BLOCK), jnp.float32)
    for n, (i, j) in enumerate(PAIRS):
        if i == j:
            diagonal += jnp.where(eye, g_ref[n], 0.0)
    jitter = (GRAM_JITTER / RANK) * jnp.sum(diagonal)
    s_ref[...] = jnp.zeros_like(s_ref)
    for n, (i, j) in enumerate(PAIRS):
        x = g_ref[n]
        if i == j:
            x = x + jnp.where(eye, jitter, 0.0)
        s_ref[BLOCK * i : BLOCK * (i + 1), BLOCK * j : BLOCK * (j + 1)] = x

    def block(b, carry):
        lo = pl.multiple_of(b * BLOCK, BLOCK)
        rows = [s_ref[pl.ds(lo + SUB * q, SUB), pl.ds(lo, BLOCK)] for q in range(GROUPS)]
        inv = [jnp.where(lane == sub + SUB * q, 1.0, 0.0) for q in range(GROUPS)]
        for q, x in enumerate(factor_block(rows, inv)):
            d_ref[SUB * q : SUB * (q + 1), :] = x
        m_bb = d_ref[...]
        s_ref[pl.ds(lo, BLOCK), :] = jnp.dot(
            m_bb, s_ref[pl.ds(lo, BLOCK), :], precision=HIGHEST, preferred_element_type=jnp.float32
        )
        s_ref[pl.ds(lo, BLOCK), pl.ds(lo, BLOCK)] = m_bb
        for i in range(1, BLOCKS):

            @pl.when(i > b)
            def _():
                here = slice(BLOCK * i, BLOCK * (i + 1))
                s_ref[here, pl.ds(lo, BLOCK)] = jnp.zeros((BLOCK, BLOCK), jnp.float32)
                s_ref[here, :] -= lax.dot_general(
                    s_ref[pl.ds(lo, BLOCK), here],
                    s_ref[pl.ds(lo, BLOCK), :],
                    (((0,), (0,)), ((), ())),
                    precision=HIGHEST,
                    preferred_element_type=jnp.float32,
                )

        return carry

    lax.fori_loop(0, BLOCKS, block, 0)
    for i in range(BLOCKS):
        for j in range(BLOCKS):
            here = (slice(BLOCK * i, BLOCK * (i + 1)), slice(BLOCK * j, BLOCK * (j + 1)))
            m_ref[here] = s_ref[here] if j <= i else jnp.zeros((BLOCK, BLOCK), jnp.float32)


def gram_kernel(p_ref, o_ref):
    for i in range(BLOCKS):
        rows = lax.dot_general(
            p_ref[:, BLOCK * i : BLOCK * (i + 1)],
            p_ref[:, BLOCK * i :],
            (((0,), (0,)), ((), ())),
            precision=HIGHEST,
            preferred_element_type=jnp.float32,
        )
        for j in range(i, BLOCKS):
            o_ref[PAIRS.index((i, j))] = rows[:, BLOCK * (j - i) : BLOCK * (j - i + 1)]


def gram_blocks(projected):
    return pl.pallas_call(
        gram_kernel,
        out_shape=jax.ShapeDtypeStruct((len(PAIRS), BLOCK, BLOCK), jnp.float32),
        in_specs=[pl.BlockSpec(memory_space=pltpu.VMEM)],
        out_specs=pl.BlockSpec(memory_space=pltpu.VMEM),
        compiler_params=pltpu.CompilerParams(vmem_limit_bytes=16 * 1024 * 1024),
        cost_estimate=pl.CostEstimate(flops=2**31, bytes_accessed=2**21, transcendentals=0),
    )(projected)


def inverse_factor(blocks):
    return pl.pallas_call(
        inverse_factor_kernel,
        out_shape=jax.ShapeDtypeStruct((RANK, RANK), jnp.float32),
        in_specs=[pl.BlockSpec(memory_space=pltpu.VMEM)],
        out_specs=pl.BlockSpec(memory_space=pltpu.VMEM),
        scratch_shapes=[pltpu.VMEM((RANK, RANK), jnp.float32), pltpu.VMEM((BLOCK, BLOCK), jnp.float32)],
        compiler_params=pltpu.CompilerParams(vmem_limit_bytes=16 * 1024 * 1024),
        cost_estimate=pl.CostEstimate(flops=2**34, bytes_accessed=2**21, transcendentals=0),
    )(blocks)


def scatter_sum(x, axis, size):
    parts = x.reshape((size, x.shape[0] // size) + x.shape[1:])
    return jnp.sum(lax.all_to_all(parts, axis, 0, 0), axis=0)


def exchange(x, axis, groups, size):
    return lax.all_to_all(jnp.broadcast_to(x, (size,) + x.shape), axis, 0, 0, axis_index_groups=groups)


def split3(x):
    hi = lax.reduce_precision(x, 8, 7)
    rest = x - hi
    mid = lax.reduce_precision(rest, 8, 7)
    return hi.astype(jnp.bfloat16), mid.astype(jnp.bfloat16), (rest - mid).astype(jnp.bfloat16)


def local(momentum, gradient, right_factor):
    n_col = lax.axis_size("col")
    n_row = lax.axis_size("row")
    n_z = n_row // 2
    core = lax.axis_index("row") % 2
    other = [(i, i ^ 1) for i in range(n_row)]
    along_z = [[2 * z + c for z in range(n_z)] for c in range(2)]

    def my_half(x):
        halves = x.reshape((2, x.shape[0] // 2) + x.shape[1:])
        mine = lax.dynamic_index_in_dim(halves, core, 0, keepdims=False)
        return mine + lax.ppermute(lax.dynamic_index_in_dim(halves, 1 - core, 0, keepdims=False), "row", other)

    def both_halves(mine):
        theirs = lax.ppermute(mine, "row", other)
        return jnp.concatenate([jnp.where(core == 0, mine, theirs), jnp.where(core == 0, theirs, mine)])

    blended = (momentum.astype(jnp.float32) + gradient.astype(jnp.float32)).astype(jnp.bfloat16)
    partial_proj = jnp.dot(blended, right_factor, preferred_element_type=jnp.float32)
    projected = exchange(scatter_sum(partial_proj, "col", n_col), "col", None, n_col).reshape(partial_proj.shape)

    packed = gram_blocks(projected).reshape(len(PAIRS) * BLOCK, BLOCK)
    share = packed.shape[0] // n_col
    packed = lax.dynamic_slice_in_dim(packed, lax.axis_index("col") * share, share, 0)
    packed = packed + lax.ppermute(packed, "row", other)
    packed, projected = lax.optimization_barrier((packed, projected))
    packed = jnp.sum(exchange(packed, "row", along_z, n_z), axis=0)
    packed = exchange(packed, "col", None, n_col).reshape(len(PAIRS), BLOCK, BLOCK)

    weights = 0.0
    for piece in split3(projected):
        weights += lax.dot_general(
            blended, piece, (((0,), (0,)), ((), ())), preferred_element_type=jnp.float32
        )
    weights = lax.psum_scatter(
        my_half(weights), "row", scatter_dimension=0, axis_index_groups=along_z, tiled=True
    )

    inverse = inverse_factor(packed)
    back_rows = jnp.dot(weights, inverse.T, precision=HIGHEST, preferred_element_type=jnp.float32)
    right_bf = lax.all_gather(
        back_rows.astype(jnp.bfloat16), "row", axis_index_groups=along_z, tiled=True
    )
    right_bf = both_halves(right_bf)
    squares = jnp.sum(back_rows * back_rows, axis=0).reshape(BLOCKS, BLOCK)
    squares = jnp.sum(exchange(squares, "col", None, n_col), axis=0)
    squares = jnp.sum(exchange(squares, "row", None, n_row), axis=0)
    back_squares = squares.reshape(RANK)
    left_bf = jnp.dot(
        projected, inverse.T, precision=HIGHEST, preferred_element_type=jnp.float32
    ).astype(jnp.bfloat16)
    new_factor = right_bf.astype(jnp.float32) / jnp.sqrt(back_squares / COLS + NORM_EPS)
    factor_bf = new_factor.astype(jnp.bfloat16)
    correction = lax.dot_general(
        left_bf, right_bf, (((1,), (1,)), ((), ())), preferred_element_type=jnp.float32
    )
    new_momentum = (blended.astype(jnp.float32) - FEEDBACK * correction).astype(jnp.bfloat16)
    update_full = lax.dot_general(
        left_bf, factor_bf, (((1,), (1,)), ((), ())), preferred_element_type=jnp.float32
    )
    weight_update = (update_full * math.sqrt(ROWS / RANK)).astype(jnp.bfloat16)
    return (new_momentum, weight_update, new_factor)


def solution(mesh):
    placed = (P("row", "col"), P("row", "col"), P("col", None))
    return jax.shard_map(
        local,
        mesh=mesh,
        in_specs=placed,
        out_specs=(P("row", "col"), P("row", "col"), P("col", None)),
        check_vma=False,
    )
```

```python
import math

import jax
import jax.numpy as jnp
from jax import lax
from jax.experimental import pallas as pl
from jax.experimental.pallas import tpu as pltpu
from jax.sharding import PartitionSpec as P

ROWS = 8192
COLS = 26624
RANK = 512


NORM_EPS = 1e-06
GRAM_JITTER = 0.0001
FEEDBACK = 0.25

HIGHEST = lax.Precision.HIGHEST
BLOCK = 128
BLOCKS = RANK // BLOCK
SUB = 8
GROUPS = BLOCK // SUB
PAIRS = [(i, j) for i in range(BLOCKS) for j in range(i, BLOCKS)]


def sub_row(x, k):
    return jnp.broadcast_to(x[k : k + 1, :], (SUB, BLOCK))


def lane_col(x, c):
    return jnp.broadcast_to(x[:, c : c + 1], (SUB, BLOCK))


def inverse_of(d):
    r = pl.reciprocal(d, approx=True)
    r = r * (2.0 - d * r)
    return r * (2.0 - d * r)


def factor_block(rows, inv):
    sub = lax.broadcasted_iota(jnp.int32, (SUB, BLOCK), 0)
    out = []
    for p in range(GROUPS):
        cols = [lane_col(rows[p], SUB * p + j) for j in range(SUB)]
        pivots, recips, row_k, inv_k, upper = [], [], [], [], []
        for k in range(SUB):
            pivot = sub_row(cols[k], k)
            r = inverse_of(pivot)
            m = jnp.where(sub > k, cols[k] * r, 0.0)
            u = {j: sub_row(cols[j], k) for j in range(k + 1, SUB)}
            for j in range(k + 1, SUB):
                cols[j] = cols[j] - m * u[j]
            vk, ek = sub_row(rows[p], k), sub_row(inv[p], k)
            if k < SUB - 1:
                rows[p] = rows[p] - m * vk
                inv[p] = inv[p] - m * ek
            pivots.append(pivot)
            recips.append(r)
            row_k.append(vk)
            inv_k.append(ek)
            upper.append(u)
        d8 = pivots[0]
        for k in range(1, SUB):
            d8 = jnp.where(sub == k, pivots[k], d8)
        out.append(inv[p] * lax.rsqrt(d8))
        for q in range(p + 1, GROUPS):
            b = [lane_col(rows[q], SUB * p + j) for j in range(SUB)]
            for k in range(SUB):
                m = b[k] * recips[k]
                for j in range(k + 1, SUB):
                    b[j] = b[j] - m * upper[k][j]
                rows[q] = rows[q] - m * row_k[k]
                inv[q] = inv[q] - m * inv_k[k]
    return out


def inverse_factor_kernel(g_ref, m_ref, s_ref, d_ref):
    lane = lax.broadcasted_iota(jnp.int32, (SUB, BLOCK), 1)
    sub = lax.broadcasted_iota(jnp.int32, (SUB, BLOCK), 0)
    eye = (
        lax.broadcasted_iota(jnp.int32, (BLOCK, BLOCK), 0)
        == lax.broadcasted_iota(jnp.int32, (BLOCK, BLOCK), 1)
    )
    diagonal = jnp.zeros((BLOCK, BLOCK), jnp.float32)
    for n, (i, j) in enumerate(PAIRS):
        if i == j:
            diagonal += jnp.where(eye, g_ref[n], 0.0)
    jitter = (GRAM_JITTER / RANK) * jnp.sum(diagonal)
    s_ref[...] = jnp.zeros_like(s_ref)
    for n, (i, j) in enumerate(PAIRS):
        x = g_ref[n]
        if i == j:
            x = x + jnp.where(eye, jitter, 0.0)
        s_ref[BLOCK * i : BLOCK * (i + 1), BLOCK * j : BLOCK * (j + 1)] = x

    def block(b, carry):
        lo = pl.multiple_of(b * BLOCK, BLOCK)
        rows = [s_ref[pl.ds(lo + SUB * q, SUB), pl.ds(lo, BLOCK)] for q in range(GROUPS)]
        inv = [jnp.where(lane == sub + SUB * q, 1.0, 0.0) for q in range(GROUPS)]
        for q, x in enumerate(factor_block(rows, inv)):
            d_ref[SUB * q : SUB * (q + 1), :] = x
        m_bb = d_ref[...]
        s_ref[pl.ds(lo, BLOCK), :] = jnp.dot(
            m_bb, s_ref[pl.ds(lo, BLOCK), :], precision=HIGHEST, preferred_element_type=jnp.float32
        )
        s_ref[pl.ds(lo, BLOCK), pl.ds(lo, BLOCK)] = m_bb
        for i in range(1, BLOCKS):

            @pl.when(i > b)
            def _():
                here = slice(BLOCK * i, BLOCK * (i + 1))
                s_ref[here, pl.ds(lo, BLOCK)] = jnp.zeros((BLOCK, BLOCK), jnp.float32)
                s_ref[here, :] -= lax.dot_general(
                    s_ref[pl.ds(lo, BLOCK), here],
                    s_ref[pl.ds(lo, BLOCK), :],
                    (((0,), (0,)), ((), ())),
                    precision=HIGHEST,
                    preferred_element_type=jnp.float32,
                )

        return carry

    lax.fori_loop(0, BLOCKS, block, 0)
    for i in range(BLOCKS):
        for j in range(BLOCKS):
            here = (slice(BLOCK * i, BLOCK * (i + 1)), slice(BLOCK * j, BLOCK * (j + 1)))
            m_ref[here] = s_ref[here] if j <= i else jnp.zeros((BLOCK, BLOCK), jnp.float32)


def gram_kernel(p_ref, o_ref):
    for i in range(BLOCKS):
        rows = lax.dot_general(
            p_ref[:, BLOCK * i : BLOCK * (i + 1)],
            p_ref[:, BLOCK * i :],
            (((0,), (0,)), ((), ())),
            precision=HIGHEST,
            preferred_element_type=jnp.float32,
        )
        for j in range(i, BLOCKS):
            o_ref[PAIRS.index((i, j))] = rows[:, BLOCK * (j - i) : BLOCK * (j - i + 1)]


def gram_blocks(projected):
    return pl.pallas_call(
        gram_kernel,
        out_shape=jax.ShapeDtypeStruct((len(PAIRS), BLOCK, BLOCK), jnp.float32),
        in_specs=[pl.BlockSpec(memory_space=pltpu.VMEM)],
        out_specs=pl.BlockSpec(memory_space=pltpu.VMEM),
        compiler_params=pltpu.CompilerParams(vmem_limit_bytes=16 * 1024 * 1024),
        cost_estimate=pl.CostEstimate(flops=2**31, bytes_accessed=2**21, transcendentals=0),
    )(projected)


def inverse_factor(blocks):
    return pl.pallas_call(
        inverse_factor_kernel,
        out_shape=jax.ShapeDtypeStruct((RANK, RANK), jnp.float32),
        in_specs=[pl.BlockSpec(memory_space=pltpu.VMEM)],
        out_specs=pl.BlockSpec(memory_space=pltpu.VMEM),
        scratch_shapes=[pltpu.VMEM((RANK, RANK), jnp.float32), pltpu.VMEM((BLOCK, BLOCK), jnp.float32)],
        compiler_params=pltpu.CompilerParams(vmem_limit_bytes=16 * 1024 * 1024),
        cost_estimate=pl.CostEstimate(flops=2**37, bytes_accessed=2**21, transcendentals=0),
    )(blocks)


def scatter_sum(x, axis, size):
    parts = x.reshape((size, x.shape[0] // size) + x.shape[1:])
    return jnp.sum(lax.all_to_all(parts, axis, 0, 0), axis=0)


def exchange(x, axis, groups, size):
    return lax.all_to_all(jnp.broadcast_to(x, (size,) + x.shape), axis, 0, 0, axis_index_groups=groups)


def split3(x):
    hi = lax.reduce_precision(x, 8, 7)
    rest = x - hi
    mid = lax.reduce_precision(rest, 8, 7)
    return hi.astype(jnp.bfloat16), mid.astype(jnp.bfloat16), (rest - mid).astype(jnp.bfloat16)


def local(momentum, gradient, right_factor):
    n_col = lax.axis_size("col")
    n_row = lax.axis_size("row")
    n_z = n_row // 2
    core = lax.axis_index("row") % 2
    other = [(i, i ^ 1) for i in range(n_row)]
    along_z = [[2 * z + c for z in range(n_z)] for c in range(2)]

    def my_half(x):
        halves = x.reshape((2, x.shape[0] // 2) + x.shape[1:])
        mine = lax.dynamic_index_in_dim(halves, core, 0, keepdims=False)
        return mine + lax.ppermute(lax.dynamic_index_in_dim(halves, 1 - core, 0, keepdims=False), "row", other)

    def both_halves(mine):
        theirs = lax.ppermute(mine, "row", other)
        return jnp.concatenate([jnp.where(core == 0, mine, theirs), jnp.where(core == 0, theirs, mine)])

    blended = (momentum.astype(jnp.float32) + gradient.astype(jnp.float32)).astype(jnp.bfloat16)
    partial_proj = jnp.dot(blended, right_factor, preferred_element_type=jnp.float32)
    projected = exchange(scatter_sum(partial_proj, "col", n_col), "col", None, n_col).reshape(partial_proj.shape)

    packed = gram_blocks(projected).reshape(len(PAIRS) * BLOCK, BLOCK)
    share = packed.shape[0] // n_col
    packed = lax.dynamic_slice_in_dim(packed, lax.axis_index("col") * share, share, 0)
    packed = packed + lax.ppermute(packed, "row", other)
    packed = jnp.sum(exchange(packed, "row", along_z, n_z), axis=0)
    packed, projected = lax.optimization_barrier((packed, projected))
    packed = exchange(packed, "col", None, n_col).reshape(len(PAIRS), BLOCK, BLOCK)

    weights = 0.0
    for piece in split3(projected):
        weights += lax.dot_general(
            blended, piece, (((0,), (0,)), ((), ())), preferred_element_type=jnp.float32
        )
    weights = lax.psum_scatter(
        my_half(weights), "row", scatter_dimension=0, axis_index_groups=along_z, tiled=True
    )

    inverse = inverse_factor(packed)
    back_rows = jnp.dot(weights, inverse.T, precision=HIGHEST, preferred_element_type=jnp.float32)
    right_bf = lax.all_gather(
        back_rows.astype(jnp.bfloat16), "row", axis_index_groups=along_z, tiled=True
    )
    right_bf = both_halves(right_bf)
    back = right_bf.astype(jnp.float32)
    squares = jnp.sum(back * back, axis=0).reshape(BLOCKS, BLOCK)
    back_squares = jnp.sum(exchange(squares, "col", None, n_col), axis=0).reshape(RANK)
    left_bf = jnp.dot(
        projected, inverse.T, precision=HIGHEST, preferred_element_type=jnp.float32
    ).astype(jnp.bfloat16)
    new_factor = back / jnp.sqrt(back_squares / COLS + NORM_EPS)
    factor_bf = new_factor.astype(jnp.bfloat16)
    correction = lax.dot_general(
        left_bf, right_bf, (((1,), (1,)), ((), ())), preferred_element_type=jnp.float32
    )
    new_momentum = (blended.astype(jnp.float32) - FEEDBACK * correction).astype(jnp.bfloat16)
    update_full = lax.dot_general(
        left_bf, factor_bf, (((1,), (1,)), ((), ())), preferred_element_type=jnp.float32
    )
    weight_update = (update_full * math.sqrt(ROWS / RANK)).astype(jnp.bfloat16)
    return (new_momentum, weight_update, new_factor)


def solution(mesh):
    placed = (P("row", "col"), P("row", "col"), P("col", None))
    return jax.shard_map(
        local,
        mesh=mesh,
        in_specs=placed,
        out_specs=(P("row", "col"), P("row", "col"), P("col", None)),
        check_vma=False,
    )
```

```python
import math

import jax
import jax.numpy as jnp
from jax import lax
from jax.experimental import pallas as pl
from jax.experimental.pallas import tpu as pltpu
from jax.sharding import PartitionSpec as P

ROWS = 8192
COLS = 26624
RANK = 512


NORM_EPS = 1e-06
GRAM_JITTER = 0.0001
FEEDBACK = 0.25

HIGHEST = lax.Precision.HIGHEST
BLOCK = 128
BLOCKS = RANK // BLOCK
SUB = 8
GROUPS = BLOCK // SUB
PAIRS = [(i, j) for i in range(BLOCKS) for j in range(i, BLOCKS)]


def sub_row(x, k):
    return jnp.broadcast_to(x[k : k + 1, :], (SUB, BLOCK))


def lane_col(x, c):
    return jnp.broadcast_to(x[:, c : c + 1], (SUB, BLOCK))


def inverse_of(d):
    r = pl.reciprocal(d, approx=True)
    r = r * (2.0 - d * r)
    return r * (2.0 - d * r)


def factor_block(rows, inv):
    sub = lax.broadcasted_iota(jnp.int32, (SUB, BLOCK), 0)
    out = []
    for p in range(GROUPS):
        cols = [lane_col(rows[p], SUB * p + j) for j in range(SUB)]
        pivots, recips, row_k, inv_k, upper = [], [], [], [], []
        for k in range(SUB):
            pivot = sub_row(cols[k], k)
            r = inverse_of(pivot)
            m = jnp.where(sub > k, cols[k] * r, 0.0)
            u = {j: sub_row(cols[j], k) for j in range(k + 1, SUB)}
            for j in range(k + 1, SUB):
                cols[j] = cols[j] - m * u[j]
            vk, ek = sub_row(rows[p], k), sub_row(inv[p], k)
            if k < SUB - 1:
                rows[p] = rows[p] - m * vk
                inv[p] = inv[p] - m * ek
            pivots.append(pivot)
            recips.append(r)
            row_k.append(vk)
            inv_k.append(ek)
            upper.append(u)
        d8 = pivots[0]
        for k in range(1, SUB):
            d8 = jnp.where(sub == k, pivots[k], d8)
        out.append(inv[p] * lax.rsqrt(d8))
        for q in range(p + 1, GROUPS):
            b = [lane_col(rows[q], SUB * p + j) for j in range(SUB)]
            for k in range(SUB):
                m = b[k] * recips[k]
                for j in range(k + 1, SUB):
                    b[j] = b[j] - m * upper[k][j]
                rows[q] = rows[q] - m * row_k[k]
                inv[q] = inv[q] - m * inv_k[k]
    return out


def inverse_factor_kernel(g_ref, m_ref, s_ref, d_ref):
    lane = lax.broadcasted_iota(jnp.int32, (SUB, BLOCK), 1)
    sub = lax.broadcasted_iota(jnp.int32, (SUB, BLOCK), 0)
    eye = (
        lax.broadcasted_iota(jnp.int32, (BLOCK, BLOCK), 0)
        == lax.broadcasted_iota(jnp.int32, (BLOCK, BLOCK), 1)
    )
    diagonal = jnp.zeros((BLOCK, BLOCK), jnp.float32)
    for n, (i, j) in enumerate(PAIRS):
        if i == j:
            diagonal += jnp.where(eye, g_ref[n], 0.0)
    jitter = (GRAM_JITTER / RANK) * jnp.sum(diagonal)
    s_ref[...] = jnp.zeros_like(s_ref)
    for n, (i, j) in enumerate(PAIRS):
        x = g_ref[n]
        if i == j:
            x = x + jnp.where(eye, jitter, 0.0)
        s_ref[BLOCK * i : BLOCK * (i + 1), BLOCK * j : BLOCK * (j + 1)] = x

    def block(b, carry):
        lo = pl.multiple_of(b * BLOCK, BLOCK)
        rows = [s_ref[pl.ds(lo + SUB * q, SUB), pl.ds(lo, BLOCK)] for q in range(GROUPS)]
        inv = [jnp.where(lane == sub + SUB * q, 1.0, 0.0) for q in range(GROUPS)]
        for q, x in enumerate(factor_block(rows, inv)):
            d_ref[SUB * q : SUB * (q + 1), :] = x
        m_bb = d_ref[...]
        s_ref[pl.ds(lo, BLOCK), :] = jnp.dot(
            m_bb, s_ref[pl.ds(lo, BLOCK), :], precision=HIGHEST, preferred_element_type=jnp.float32
        )
        s_ref[pl.ds(lo, BLOCK), pl.ds(lo, BLOCK)] = m_bb
        for i in range(1, BLOCKS):

            @pl.when(i > b)
            def _():
                here = slice(BLOCK * i, BLOCK * (i + 1))
                s_ref[here, pl.ds(lo, BLOCK)] = jnp.zeros((BLOCK, BLOCK), jnp.float32)
                s_ref[here, :] -= lax.dot_general(
                    s_ref[pl.ds(lo, BLOCK), here],
                    s_ref[pl.ds(lo, BLOCK), :],
                    (((0,), (0,)), ((), ())),
                    precision=HIGHEST,
                    preferred_element_type=jnp.float32,
                )

        return carry

    lax.fori_loop(0, BLOCKS, block, 0)
    for i in range(BLOCKS):
        for j in range(BLOCKS):
            here = (slice(BLOCK * i, BLOCK * (i + 1)), slice(BLOCK * j, BLOCK * (j + 1)))
            m_ref[here] = s_ref[here] if j <= i else jnp.zeros((BLOCK, BLOCK), jnp.float32)


def gram_kernel(p_ref, o_ref):
    for i in range(BLOCKS):
        rows = lax.dot_general(
            p_ref[:, BLOCK * i : BLOCK * (i + 1)],
            p_ref[:, BLOCK * i :],
            (((0,), (0,)), ((), ())),
            precision=HIGHEST,
            preferred_element_type=jnp.float32,
        )
        for j in range(i, BLOCKS):
            o_ref[PAIRS.index((i, j))] = rows[:, BLOCK * (j - i) : BLOCK * (j - i + 1)]


def gram_blocks(projected):
    return pl.pallas_call(
        gram_kernel,
        out_shape=jax.ShapeDtypeStruct((len(PAIRS), BLOCK, BLOCK), jnp.float32),
        in_specs=[pl.BlockSpec(memory_space=pltpu.VMEM)],
        out_specs=pl.BlockSpec(memory_space=pltpu.VMEM),
        compiler_params=pltpu.CompilerParams(vmem_limit_bytes=16 * 1024 * 1024),
        cost_estimate=pl.CostEstimate(flops=2**31, bytes_accessed=2**21, transcendentals=0),
    )(projected)


def inverse_factor(blocks):
    return pl.pallas_call(
        inverse_factor_kernel,
        out_shape=jax.ShapeDtypeStruct((RANK, RANK), jnp.float32),
        in_specs=[pl.BlockSpec(memory_space=pltpu.VMEM)],
        out_specs=pl.BlockSpec(memory_space=pltpu.VMEM),
        scratch_shapes=[pltpu.VMEM((RANK, RANK), jnp.float32), pltpu.VMEM((BLOCK, BLOCK), jnp.float32)],
        compiler_params=pltpu.CompilerParams(vmem_limit_bytes=16 * 1024 * 1024),
        cost_estimate=pl.CostEstimate(flops=2**37, bytes_accessed=2**21, transcendentals=0),
    )(blocks)


def weights_kernel(core_ref, b_ref, p_ref, mine_ref, theirs_ref, w_ref):
    rest = p_ref[...]
    for n in range(3):
        piece = rest.astype(jnp.bfloat16)
        rest = rest - piece.astype(jnp.float32)
        term = lax.dot_general(
            b_ref[...], piece, (((0,), (0,)), ((), ())), preferred_element_type=jnp.float32
        )
        w_ref[...] = term if n == 0 else w_ref[...] + term
    half = mine_ref.shape[0]
    core = core_ref[0]
    mine_ref[...] = w_ref[pl.ds(pl.multiple_of(core * half, SUB), half), :]
    theirs_ref[...] = w_ref[pl.ds(pl.multiple_of((1 - core) * half, SUB), half), :]


def weights_halves(core, blended, projected):
    half = jax.ShapeDtypeStruct((blended.shape[1] // 2, RANK), jnp.float32)
    return pl.pallas_call(
        weights_kernel,
        out_shape=(half, half),
        in_specs=[
            pl.BlockSpec(memory_space=pltpu.SMEM),
            pl.BlockSpec(memory_space=pltpu.VMEM),
            pl.BlockSpec(memory_space=pltpu.VMEM),
        ],
        out_specs=(pl.BlockSpec(memory_space=pltpu.VMEM), pl.BlockSpec(memory_space=pltpu.VMEM)),
        scratch_shapes=[pltpu.VMEM((blended.shape[1], RANK), jnp.float32)],
        compiler_params=pltpu.CompilerParams(vmem_limit_bytes=32 * 1024 * 1024),
        cost_estimate=pl.CostEstimate(flops=2**32, bytes_accessed=2**22, transcendentals=0),
    )(core.astype(jnp.int32).reshape(1), blended, projected)


def scatter_sum(x, axis, size):
    parts = x.reshape((size, x.shape[0] // size) + x.shape[1:])
    return jnp.sum(lax.all_to_all(parts, axis, 0, 0), axis=0)


def exchange(x, axis, groups, size):
    return lax.all_to_all(jnp.broadcast_to(x, (size,) + x.shape), axis, 0, 0, axis_index_groups=groups)


def local(momentum, gradient, right_factor):
    n_col = lax.axis_size("col")
    n_row = lax.axis_size("row")
    n_z = n_row // 2
    core = lax.axis_index("row") % 2
    other = [(i, i ^ 1) for i in range(n_row)]
    along_z = [[2 * z + c for z in range(n_z)] for c in range(2)]

    def both_halves(mine):
        theirs = lax.ppermute(mine, "row", other)
        return jnp.concatenate([jnp.where(core == 0, mine, theirs), jnp.where(core == 0, theirs, mine)])

    blended = (momentum.astype(jnp.float32) + gradient.astype(jnp.float32)).astype(jnp.bfloat16)
    partial_proj = jnp.dot(blended, right_factor, preferred_element_type=jnp.float32)
    projected = exchange(scatter_sum(partial_proj, "col", n_col), "col", None, n_col).reshape(partial_proj.shape)

    packed = gram_blocks(projected).reshape(len(PAIRS) * BLOCK, BLOCK)
    share = packed.shape[0] // n_col
    packed = lax.dynamic_slice_in_dim(packed, lax.axis_index("col") * share, share, 0)
    packed = packed + lax.ppermute(packed, "row", other)
    packed, projected = lax.optimization_barrier((packed, projected))
    packed = jnp.sum(exchange(packed, "row", along_z, n_z), axis=0)
    packed = exchange(packed, "col", None, n_col).reshape(len(PAIRS), BLOCK, BLOCK)

    mine, theirs = weights_halves(core, blended, projected)
    weights = lax.psum_scatter(
        mine + lax.ppermute(theirs, "row", other),
        "row",
        scatter_dimension=0,
        axis_index_groups=along_z,
        tiled=True,
    )

    inverse = inverse_factor(packed)
    back_rows = jnp.dot(weights, inverse.T, precision=HIGHEST, preferred_element_type=jnp.float32)
    right_bf = lax.all_gather(
        back_rows.astype(jnp.bfloat16), "row", axis_index_groups=along_z, tiled=True
    )
    right_bf = both_halves(right_bf)
    back = right_bf.astype(jnp.float32)
    squares = jnp.sum(back * back, axis=0).reshape(BLOCKS, BLOCK)
    squares, projected, inverse = lax.optimization_barrier((squares, projected, inverse))
    back_squares = jnp.sum(exchange(squares, "col", None, n_col), axis=0).reshape(RANK)
    left_bf = jnp.dot(
        projected, inverse.T, precision=HIGHEST, preferred_element_type=jnp.float32
    ).astype(jnp.bfloat16)
    new_factor = back / jnp.sqrt(back_squares / COLS + NORM_EPS)
    factor_bf = new_factor.astype(jnp.bfloat16)
    correction = lax.dot_general(
        left_bf, right_bf, (((1,), (1,)), ((), ())), preferred_element_type=jnp.float32
    )
    new_momentum = (blended.astype(jnp.float32) - FEEDBACK * correction).astype(jnp.bfloat16)
    update_full = lax.dot_general(
        left_bf, factor_bf, (((1,), (1,)), ((), ())), preferred_element_type=jnp.float32
    )
    weight_update = (update_full * math.sqrt(ROWS / RANK)).astype(jnp.bfloat16)
    return (new_momentum, weight_update, new_factor)


def solution(mesh):
    placed = (P("row", "col"), P("row", "col"), P("col", None))
    return jax.shard_map(
        local,
        mesh=mesh,
        in_specs=placed,
        out_specs=(P("row", "col"), P("row", "col"), P("col", None)),
        check_vma=False,
    )
```

```python
import math

import jax
import jax.numpy as jnp
from jax import lax
from jax.experimental import pallas as pl
from jax.experimental.pallas import tpu as pltpu
from jax.sharding import PartitionSpec as P

ROWS = 8192
COLS = 26624
RANK = 512


NORM_EPS = 1e-06
GRAM_JITTER = 0.0001
FEEDBACK = 0.25

HIGHEST = lax.Precision.HIGHEST
BLOCK = 128
BLOCKS = RANK // BLOCK
SUB = 8
GROUPS = BLOCK // SUB
PAIRS = [(i, j) for i in range(BLOCKS) for j in range(i, BLOCKS)]


def sub_row(x, k):
    return jnp.broadcast_to(x[k : k + 1, :], (SUB, BLOCK))


def lane_col(x, c):
    return jnp.broadcast_to(x[:, c : c + 1], (SUB, BLOCK))


def pieces(x):
    hi = x.astype(jnp.bfloat16)
    rest = x - hi.astype(jnp.float32)
    mid = rest.astype(jnp.bfloat16)
    return hi, mid, (rest - mid.astype(jnp.float32)).astype(jnp.bfloat16)


def stacked(*parts):
    return jnp.concatenate([x.astype(jnp.float32) for x in parts], axis=0).astype(jnp.bfloat16)


def factor_block(rows):
    sub = lax.broadcasted_iota(jnp.int32, (SUB, BLOCK), 0)
    lane = lax.broadcasted_iota(jnp.int32, (SUB, BLOCK), 1)
    out = []
    for p in range(GROUPS):
        panel = (lane >= SUB * p) & (lane < SUB * (p + 1))
        cols = [lane_col(rows[p], SUB * p + j) for j in range(SUB)]
        x = jnp.where(panel, jnp.where(lane == sub + SUB * p, 1.0, 0.0), rows[p])
        pivots, recips, row_k, upper = [], [], [], []
        for k in range(SUB):
            pivot = sub_row(cols[k], k)
            r = pl.reciprocal(pivot, approx=True)
            m = jnp.where(sub > k, cols[k] * r, 0.0)
            u = {j: sub_row(cols[j], k) for j in range(k + 1, SUB)}
            for j in range(k + 1, SUB):
                cols[j] = cols[j] - m * u[j]
            xk = sub_row(x, k)
            if k < SUB - 1:
                x = x - m * xk
            pivots.append(pivot)
            recips.append(r)
            row_k.append(xk)
            upper.append(u)
        d8 = pivots[0]
        for k in range(1, SUB):
            d8 = jnp.where(sub == k, pivots[k], d8)
        out.append(jnp.where(lane < SUB * (p + 1), x * lax.rsqrt(d8), 0.0))
        if p + 1 < GROUPS:
            b = [lane_col(rows[p + 1], SUB * p + j) for j in range(SUB)]
            y = jnp.where(panel, 0.0, rows[p + 1])
            for k in range(SUB):
                m = b[k] * recips[k]
                for j in range(k + 1, SUB):
                    b[j] = b[j] - m * upper[k][j]
                y = y - m * row_k[k]
            rows[p + 1] = y
        if p + 2 < GROUPS:
            r8 = recips[0]
            for k in range(1, SUB):
                r8 = jnp.where(sub == k, recips[k], r8)
            hi, mid, low = pieces(x)
            hi2, mid2, low2 = pieces(x * r8)
            product = lax.dot_general(
                stacked(hi, hi, mid, mid, hi, low),
                stacked(hi2, mid2, hi2, mid2, low2, hi2),
                (((0,), (0,)), ((), ())),
                preferred_element_type=jnp.float32,
            )
            for q in range(p + 2, GROUPS):
                rows[q] = jnp.where(panel, 0.0, rows[q]) - product[SUB * q : SUB * (q + 1), :]
    return out


def inverse_factor_kernel(g_ref, m_ref, s_ref, d_ref, x_ref, y_ref):
    eye = (
        lax.broadcasted_iota(jnp.int32, (BLOCK, BLOCK), 0)
        == lax.broadcasted_iota(jnp.int32, (BLOCK, BLOCK), 1)
    )
    diagonal = jnp.zeros((BLOCK, BLOCK), jnp.float32)
    for n, (i, j) in enumerate(PAIRS):
        if i == j:
            diagonal += jnp.where(eye, g_ref[n], 0.0)
    jitter = (GRAM_JITTER / RANK) * jnp.sum(diagonal)
    s_ref[...] = jnp.zeros_like(s_ref)
    for n, (i, j) in enumerate(PAIRS):
        x = g_ref[n]
        if i == j:
            x = x + jnp.where(eye, jitter, 0.0)
        s_ref[BLOCK * i : BLOCK * (i + 1), BLOCK * j : BLOCK * (j + 1)] = x

    def block(b, carry):
        lo = pl.multiple_of(b * BLOCK, BLOCK)
        rows = [s_ref[pl.ds(lo + SUB * q, SUB), pl.ds(lo, BLOCK)] for q in range(GROUPS)]
        for q, x in enumerate(factor_block(rows)):
            d_ref[SUB * q : SUB * (q + 1), :] = x
        m_bb = d_ref[...]
        hi, mid, low = pieces(m_bb)
        first = jnp.concatenate([hi, hi, mid, mid, hi, low], axis=1)
        hi, mid, low = pieces(s_ref[pl.ds(lo, BLOCK), :])
        second = jnp.concatenate([hi, mid, hi, mid, low, hi], axis=0)
        s_ref[pl.ds(lo, BLOCK), :] = jnp.dot(first, second, preferred_element_type=jnp.float32)
        s_ref[pl.ds(lo, BLOCK), pl.ds(lo, BLOCK)] = m_bb
        hi, mid, low = pieces(s_ref[pl.ds(lo, BLOCK), :])
        for n, (x, y) in enumerate(((hi, hi), (hi, mid), (mid, hi), (mid, mid), (hi, low), (low, hi))):
            x_ref[BLOCK * n : BLOCK * (n + 1), :] = x
            y_ref[BLOCK * n : BLOCK * (n + 1), :] = y
        for i in range(1, BLOCKS):

            @pl.when(i > b)
            def _():
                here = slice(BLOCK * i, BLOCK * (i + 1))
                s_ref[here, pl.ds(lo, BLOCK)] = jnp.zeros((BLOCK, BLOCK), jnp.float32)
                s_ref[here, :] -= lax.dot_general(
                    x_ref[:, here], y_ref[...], (((0,), (0,)), ((), ())), preferred_element_type=jnp.float32
                )

        return carry

    lax.fori_loop(0, BLOCKS, block, 0)
    for i in range(BLOCKS):
        for j in range(BLOCKS):
            here = (slice(BLOCK * i, BLOCK * (i + 1)), slice(BLOCK * j, BLOCK * (j + 1)))
            m_ref[here] = s_ref[here] if j <= i else jnp.zeros((BLOCK, BLOCK), jnp.float32)


def gram_kernel(p_ref, o_ref):
    for i in range(BLOCKS):
        rows = lax.dot_general(
            p_ref[:, BLOCK * i : BLOCK * (i + 1)],
            p_ref[:, BLOCK * i :],
            (((0,), (0,)), ((), ())),
            precision=HIGHEST,
            preferred_element_type=jnp.float32,
        )
        for j in range(i, BLOCKS):
            o_ref[PAIRS.index((i, j))] = rows[:, BLOCK * (j - i) : BLOCK * (j - i + 1)]


def gram_blocks(projected):
    return pl.pallas_call(
        gram_kernel,
        out_shape=jax.ShapeDtypeStruct((len(PAIRS), BLOCK, BLOCK), jnp.float32),
        in_specs=[pl.BlockSpec(memory_space=pltpu.VMEM)],
        out_specs=pl.BlockSpec(memory_space=pltpu.VMEM),
        compiler_params=pltpu.CompilerParams(vmem_limit_bytes=16 * 1024 * 1024),
        cost_estimate=pl.CostEstimate(flops=2**31, bytes_accessed=2**21, transcendentals=0),
    )(projected)


def inverse_factor(blocks):
    return pl.pallas_call(
        inverse_factor_kernel,
        out_shape=jax.ShapeDtypeStruct((RANK, RANK), jnp.float32),
        in_specs=[pl.BlockSpec(memory_space=pltpu.VMEM)],
        out_specs=pl.BlockSpec(memory_space=pltpu.VMEM),
        scratch_shapes=[
            pltpu.VMEM((RANK, RANK), jnp.float32),
            pltpu.VMEM((BLOCK, BLOCK), jnp.float32),
            pltpu.VMEM((6 * BLOCK, RANK), jnp.bfloat16),
            pltpu.VMEM((6 * BLOCK, RANK), jnp.bfloat16),
        ],
        compiler_params=pltpu.CompilerParams(vmem_limit_bytes=16 * 1024 * 1024),
        cost_estimate=pl.CostEstimate(flops=2**37, bytes_accessed=2**21, transcendentals=0),
    )(blocks)


def weights_kernel(half_ref, b_ref, p_ref, *refs):
    *added, o_ref, w_ref = refs
    start = b_ref.shape[1] - w_ref.shape[0]
    half = half_ref[0]
    rows = b_ref[:, pl.ds(pl.multiple_of(half * start, BLOCK), w_ref.shape[0])]
    for n, piece in enumerate(pieces(p_ref[...])):
        term = lax.dot_general(rows, piece, (((0,), (0,)), ((), ())), preferred_element_type=jnp.float32)
        w_ref[...] = term if n == 0 else w_ref[...] + term
    own = w_ref[pl.ds(pl.multiple_of(half * (o_ref.shape[0] - start), SUB), o_ref.shape[0]), :]
    o_ref[...] = own + added[0][...] if added else own


def weights_half(half, blended, projected, *added):
    rows = blended.shape[1] // 2
    start = rows // BLOCK * BLOCK
    vmem = pl.BlockSpec(memory_space=pltpu.VMEM)
    return pl.pallas_call(
        weights_kernel,
        out_shape=jax.ShapeDtypeStruct((rows, RANK), jnp.float32),
        in_specs=[pl.BlockSpec(memory_space=pltpu.SMEM)] + [vmem] * (2 + len(added)),
        out_specs=vmem,
        scratch_shapes=[pltpu.VMEM((blended.shape[1] - start, RANK), jnp.float32)],
        compiler_params=pltpu.CompilerParams(vmem_limit_bytes=32 * 1024 * 1024),
        cost_estimate=pl.CostEstimate(flops=2**31, bytes_accessed=2**22, transcendentals=0),
    )(half.astype(jnp.int32).reshape(1), blended, projected, *added)


def scatter_sum(x, axis, size):
    parts = x.reshape((size, x.shape[0] // size) + x.shape[1:])
    return jnp.sum(lax.all_to_all(parts, axis, 0, 0), axis=0)


def exchange(x, axis, groups, size):
    return lax.all_to_all(jnp.broadcast_to(x, (size,) + x.shape), axis, 0, 0, axis_index_groups=groups)


def local(momentum, gradient, right_factor):
    n_col = lax.axis_size("col")
    n_row = lax.axis_size("row")
    n_z = n_row // 2
    core = lax.axis_index("row") % 2
    other = [(i, i ^ 1) for i in range(n_row)]
    along_z = [[2 * z + c for z in range(n_z)] for c in range(2)]

    def both_halves(mine):
        theirs = lax.ppermute(mine, "row", other)
        return jnp.concatenate([jnp.where(core == 0, mine, theirs), jnp.where(core == 0, theirs, mine)])

    blended = (momentum.astype(jnp.float32) + gradient.astype(jnp.float32)).astype(jnp.bfloat16)
    partial_proj = jnp.dot(blended, right_factor, preferred_element_type=jnp.float32)
    projected = exchange(scatter_sum(partial_proj, "col", n_col), "col", None, n_col).reshape(partial_proj.shape)

    theirs = weights_half(1 - core, blended, projected)
    theirs, projected = lax.optimization_barrier((theirs, projected))
    theirs = lax.ppermute(theirs, "row", other)

    packed = gram_blocks(projected).reshape(len(PAIRS) * BLOCK, BLOCK)
    share = packed.shape[0] // n_col
    packed = lax.dynamic_slice_in_dim(packed, lax.axis_index("col") * share, share, 0)
    packed = packed + lax.ppermute(packed, "row", other)

    weights = weights_half(core, blended, projected, theirs)
    packed, weights = lax.optimization_barrier((packed, weights))
    weights = lax.psum_scatter(
        weights, "row", scatter_dimension=0, axis_index_groups=along_z, tiled=True
    )
    packed = jnp.sum(exchange(packed, "row", along_z, n_z), axis=0)
    packed = exchange(packed, "col", None, n_col).reshape(len(PAIRS), BLOCK, BLOCK)

    inverse = inverse_factor(packed)
    back_rows = jnp.dot(weights, inverse.T, precision=HIGHEST, preferred_element_type=jnp.float32)
    right_bf = lax.all_gather(
        back_rows.astype(jnp.bfloat16), "row", axis_index_groups=along_z, tiled=True
    )
    right_bf = both_halves(right_bf)
    back = right_bf.astype(jnp.float32)
    squares = jnp.sum(back * back, axis=0).reshape(BLOCKS, BLOCK)
    squares, projected, inverse = lax.optimization_barrier((squares, projected, inverse))
    back_squares = jnp.sum(exchange(squares, "col", None, n_col), axis=0).reshape(RANK)
    left_bf = jnp.dot(
        projected, inverse.T, precision=HIGHEST, preferred_element_type=jnp.float32
    ).astype(jnp.bfloat16)
    new_factor = back / jnp.sqrt(back_squares / COLS + NORM_EPS)
    factor_bf = new_factor.astype(jnp.bfloat16)
    correction = lax.dot_general(
        left_bf, right_bf, (((1,), (1,)), ((), ())), preferred_element_type=jnp.float32
    )
    new_momentum = (blended.astype(jnp.float32) - FEEDBACK * correction).astype(jnp.bfloat16)
    update_full = lax.dot_general(
        left_bf, factor_bf, (((1,), (1,)), ((), ())), preferred_element_type=jnp.float32
    )
    weight_update = (update_full * math.sqrt(ROWS / RANK)).astype(jnp.bfloat16)
    return (new_momentum, weight_update, new_factor)


def solution(mesh):
    placed = (P("row", "col"), P("row", "col"), P("col", None))
    return jax.shard_map(
        local,
        mesh=mesh,
        in_specs=placed,
        out_specs=(P("row", "col"), P("row", "col"), P("col", None)),
        check_vma=False,
    )
```

```python
import math

import jax
import jax.numpy as jnp
from jax import lax
from jax.experimental import pallas as pl
from jax.experimental.pallas import tpu as pltpu
from jax.sharding import PartitionSpec as P

ROWS = 8192
COLS = 26624
RANK = 512


NORM_EPS = 1e-06
GRAM_JITTER = 0.0001
FEEDBACK = 0.25

HIGHEST = lax.Precision.HIGHEST
BLOCK = 128
BLOCKS = RANK // BLOCK
SUB = 8
GROUPS = BLOCK // SUB
PAIRS = [(i, j) for i in range(BLOCKS) for j in range(i, BLOCKS)]


def sub_row(x, k):
    return jnp.broadcast_to(x[k : k + 1, :], (SUB, BLOCK))


def lane_col(x, c):
    return jnp.broadcast_to(x[:, c : c + 1], (SUB, BLOCK))


def pieces(x):
    hi = x.astype(jnp.bfloat16)
    rest = x - hi.astype(jnp.float32)
    mid = rest.astype(jnp.bfloat16)
    return hi, mid, (rest - mid.astype(jnp.float32)).astype(jnp.bfloat16)


def stacked(*parts):
    return jnp.concatenate([x.astype(jnp.float32) for x in parts], axis=0).astype(jnp.bfloat16)


def factor_block(rows):
    sub = lax.broadcasted_iota(jnp.int32, (SUB, BLOCK), 0)
    lane = lax.broadcasted_iota(jnp.int32, (SUB, BLOCK), 1)
    out = []
    for p in range(GROUPS):
        panel = (lane >= SUB * p) & (lane < SUB * (p + 1))
        cols = [lane_col(rows[p], SUB * p + j) for j in range(SUB)]
        x = jnp.where(panel, jnp.where(lane == sub + SUB * p, 1.0, 0.0), rows[p])
        pivots, recips, row_k, upper = [], [], [], []
        for k in range(SUB):
            pivot = sub_row(cols[k], k)
            r = pl.reciprocal(pivot, approx=True)
            m = jnp.where(sub > k, cols[k] * r, 0.0)
            u = {j: sub_row(cols[j], k) for j in range(k + 1, SUB)}
            for j in range(k + 1, SUB):
                cols[j] = cols[j] - m * u[j]
            xk = sub_row(x, k)
            if k < SUB - 1:
                x = x - m * xk
            pivots.append(pivot)
            recips.append(r)
            row_k.append(xk)
            upper.append(u)
        d8 = pivots[0]
        for k in range(1, SUB):
            d8 = jnp.where(sub == k, pivots[k], d8)
        out.append(jnp.where(lane < SUB * (p + 1), x * lax.rsqrt(d8), 0.0))
        if p + 1 < GROUPS:
            b = [lane_col(rows[p + 1], SUB * p + j) for j in range(SUB)]
            y = jnp.where(panel, 0.0, rows[p + 1])
            for k in range(SUB):
                m = b[k] * recips[k]
                for j in range(k + 1, SUB):
                    b[j] = b[j] - m * upper[k][j]
                y = y - m * row_k[k]
            rows[p + 1] = y
        if p + 2 < GROUPS:
            r8 = recips[0]
            for k in range(1, SUB):
                r8 = jnp.where(sub == k, recips[k], r8)
            hi, mid, low = pieces(x)
            hi2, mid2, low2 = pieces(x * r8)
            product = lax.dot_general(
                stacked(hi, hi, mid, mid, hi, low),
                stacked(hi2, mid2, hi2, mid2, low2, hi2),
                (((0,), (0,)), ((), ())),
                preferred_element_type=jnp.float32,
            )
            for q in range(p + 2, GROUPS):
                rows[q] = jnp.where(panel, 0.0, rows[q]) - product[SUB * q : SUB * (q + 1), :]
    return out


def inverse_factor_kernel(g_ref, m_ref, s_ref, d_ref, x_ref, y_ref):
    eye = (
        lax.broadcasted_iota(jnp.int32, (BLOCK, BLOCK), 0)
        == lax.broadcasted_iota(jnp.int32, (BLOCK, BLOCK), 1)
    )
    diagonal = jnp.zeros((BLOCK, BLOCK), jnp.float32)
    for n, (i, j) in enumerate(PAIRS):
        if i == j:
            diagonal += jnp.where(eye, g_ref[n], 0.0)
    jitter = (GRAM_JITTER / RANK) * jnp.sum(diagonal)
    s_ref[...] = jnp.zeros_like(s_ref)
    for n, (i, j) in enumerate(PAIRS):
        x = g_ref[n]
        if i == j:
            x = x + jnp.where(eye, jitter, 0.0)
        s_ref[BLOCK * i : BLOCK * (i + 1), BLOCK * j : BLOCK * (j + 1)] = x

    def block(b, carry):
        lo = pl.multiple_of(b * BLOCK, BLOCK)
        rows = [s_ref[pl.ds(lo + SUB * q, SUB), pl.ds(lo, BLOCK)] for q in range(GROUPS)]
        for q, x in enumerate(factor_block(rows)):
            d_ref[SUB * q : SUB * (q + 1), :] = x
        m_bb = d_ref[...]
        hi, mid, low = pieces(m_bb)
        first = jnp.concatenate([hi, hi, mid, mid, hi, low], axis=1)
        hi, mid, low = pieces(s_ref[pl.ds(lo, BLOCK), :])
        second = jnp.concatenate([hi, mid, hi, mid, low, hi], axis=0)
        s_ref[pl.ds(lo, BLOCK), :] = jnp.dot(first, second, preferred_element_type=jnp.float32)
        s_ref[pl.ds(lo, BLOCK), pl.ds(lo, BLOCK)] = m_bb
        hi, mid, low = pieces(s_ref[pl.ds(lo, BLOCK), :])
        for n, (x, y) in enumerate(((hi, hi), (hi, mid), (mid, hi), (mid, mid), (hi, low), (low, hi))):
            x_ref[BLOCK * n : BLOCK * (n + 1), :] = x
            y_ref[BLOCK * n : BLOCK * (n + 1), :] = y
        for i in range(1, BLOCKS):

            @pl.when(i > b)
            def _():
                here = slice(BLOCK * i, BLOCK * (i + 1))
                s_ref[here, pl.ds(lo, BLOCK)] = jnp.zeros((BLOCK, BLOCK), jnp.float32)
                s_ref[here, :] -= lax.dot_general(
                    x_ref[:, here], y_ref[...], (((0,), (0,)), ((), ())), preferred_element_type=jnp.float32
                )

        return carry

    lax.fori_loop(0, BLOCKS, block, 0)
    for i in range(BLOCKS):
        for j in range(BLOCKS):
            here = (slice(BLOCK * i, BLOCK * (i + 1)), slice(BLOCK * j, BLOCK * (j + 1)))
            m_ref[here] = s_ref[here] if j <= i else jnp.zeros((BLOCK, BLOCK), jnp.float32)


def gram_kernel(p_ref, o_ref):
    for i in range(BLOCKS):
        rows = lax.dot_general(
            p_ref[:, BLOCK * i : BLOCK * (i + 1)],
            p_ref[:, BLOCK * i :],
            (((0,), (0,)), ((), ())),
            precision=HIGHEST,
            preferred_element_type=jnp.float32,
        )
        for j in range(i, BLOCKS):
            o_ref[PAIRS.index((i, j))] = rows[:, BLOCK * (j - i) : BLOCK * (j - i + 1)]


def gram_blocks(projected):
    return pl.pallas_call(
        gram_kernel,
        out_shape=jax.ShapeDtypeStruct((len(PAIRS), BLOCK, BLOCK), jnp.float32),
        in_specs=[pl.BlockSpec(memory_space=pltpu.VMEM)],
        out_specs=pl.BlockSpec(memory_space=pltpu.VMEM),
        compiler_params=pltpu.CompilerParams(vmem_limit_bytes=16 * 1024 * 1024),
        cost_estimate=pl.CostEstimate(flops=2**31, bytes_accessed=2**21, transcendentals=0),
    )(projected)


def inverse_factor(blocks):
    return pl.pallas_call(
        inverse_factor_kernel,
        out_shape=jax.ShapeDtypeStruct((RANK, RANK), jnp.float32),
        in_specs=[pl.BlockSpec(memory_space=pltpu.VMEM)],
        out_specs=pl.BlockSpec(memory_space=pltpu.VMEM),
        scratch_shapes=[
            pltpu.VMEM((RANK, RANK), jnp.float32),
            pltpu.VMEM((BLOCK, BLOCK), jnp.float32),
            pltpu.VMEM((6 * BLOCK, RANK), jnp.bfloat16),
            pltpu.VMEM((6 * BLOCK, RANK), jnp.bfloat16),
        ],
        compiler_params=pltpu.CompilerParams(vmem_limit_bytes=16 * 1024 * 1024),
        cost_estimate=pl.CostEstimate(flops=26 * 10**9, bytes_accessed=2**21, transcendentals=0),
    )(blocks)


def weights_kernel(half_ref, b_ref, p_ref, *refs):
    *added, o_ref, w_ref = refs
    start = b_ref.shape[1] - w_ref.shape[0]
    half = half_ref[0]
    rows = b_ref[:, pl.ds(pl.multiple_of(half * start, BLOCK), w_ref.shape[0])]
    for n, piece in enumerate(pieces(p_ref[...])):
        term = lax.dot_general(rows, piece, (((0,), (0,)), ((), ())), preferred_element_type=jnp.float32)
        w_ref[...] = term if n == 0 else w_ref[...] + term
    own = w_ref[pl.ds(pl.multiple_of(half * (o_ref.shape[0] - start), SUB), o_ref.shape[0]), :]
    o_ref[...] = own + added[0][...] if added else own


def weights_half(half, blended, projected, *added):
    rows = blended.shape[1] // 2
    start = rows // BLOCK * BLOCK
    vmem = pl.BlockSpec(memory_space=pltpu.VMEM)
    return pl.pallas_call(
        weights_kernel,
        out_shape=jax.ShapeDtypeStruct((rows, RANK), jnp.float32),
        in_specs=[pl.BlockSpec(memory_space=pltpu.SMEM)] + [vmem] * (2 + len(added)),
        out_specs=vmem,
        scratch_shapes=[pltpu.VMEM((blended.shape[1] - start, RANK), jnp.float32)],
        compiler_params=pltpu.CompilerParams(vmem_limit_bytes=32 * 1024 * 1024),
        cost_estimate=pl.CostEstimate(flops=2**31, bytes_accessed=2**22, transcendentals=0),
    )(half.astype(jnp.int32).reshape(1), blended, projected, *added)


def scatter_sum(x, axis, size):
    parts = x.reshape((size, x.shape[0] // size) + x.shape[1:])
    return jnp.sum(lax.all_to_all(parts, axis, 0, 0), axis=0)


def exchange(x, axis, groups, size):
    return lax.all_to_all(jnp.broadcast_to(x, (size,) + x.shape), axis, 0, 0, axis_index_groups=groups)


def local(momentum, gradient, right_factor):
    n_col = lax.axis_size("col")
    n_row = lax.axis_size("row")
    n_z = n_row // 2
    core = lax.axis_index("row") % 2
    other = [(i, i ^ 1) for i in range(n_row)]
    along_z = [[2 * z + c for z in range(n_z)] for c in range(2)]

    def both_halves(mine):
        theirs = lax.ppermute(mine, "row", other)
        return jnp.concatenate([jnp.where(core == 0, mine, theirs), jnp.where(core == 0, theirs, mine)])

    blended = (momentum.astype(jnp.float32) + gradient.astype(jnp.float32)).astype(jnp.bfloat16)
    partial_proj = jnp.dot(blended, right_factor, preferred_element_type=jnp.float32)
    projected = exchange(scatter_sum(partial_proj, "col", n_col), "col", None, n_col).reshape(partial_proj.shape)

    theirs = weights_half(1 - core, blended, projected)
    theirs, projected = lax.optimization_barrier((theirs, projected))
    theirs = lax.ppermute(theirs, "row", other)

    packed = gram_blocks(projected).reshape(len(PAIRS) * BLOCK, BLOCK)
    share = packed.shape[0] // n_col
    packed = lax.dynamic_slice_in_dim(packed, lax.axis_index("col") * share, share, 0)
    packed = packed + lax.ppermute(packed, "row", other)

    weights = weights_half(core, blended, projected, theirs)
    weights = lax.psum_scatter(
        weights, "row", scatter_dimension=0, axis_index_groups=along_z, tiled=True
    )
    packed = jnp.sum(exchange(packed, "row", along_z, n_z), axis=0)
    packed = exchange(packed, "col", None, n_col).reshape(len(PAIRS), BLOCK, BLOCK)

    inverse = inverse_factor(packed)
    back_rows = jnp.dot(weights, inverse.T, precision=HIGHEST, preferred_element_type=jnp.float32)
    half = lax.all_gather(
        back_rows.astype(jnp.bfloat16), "row", axis_index_groups=along_z, tiled=True
    )
    squares = jnp.sum(jnp.square(half.astype(jnp.float32)), axis=0).reshape(BLOCKS, BLOCK)
    squares = squares + lax.ppermute(squares, "row", other)
    squares, projected, inverse = lax.optimization_barrier((squares, projected, inverse))
    squares = exchange(squares, "col", None, n_col)
    right_bf = both_halves(half)
    left_bf = jnp.dot(
        projected, inverse.T, precision=HIGHEST, preferred_element_type=jnp.float32
    ).astype(jnp.bfloat16)
    correction = lax.dot_general(
        left_bf, right_bf, (((1,), (1,)), ((), ())), preferred_element_type=jnp.float32
    )
    new_momentum = (blended.astype(jnp.float32) - FEEDBACK * correction).astype(jnp.bfloat16)
    squares, new_momentum = lax.optimization_barrier((squares, new_momentum))
    back_squares = jnp.sum(squares, axis=0).reshape(RANK)
    new_factor = right_bf.astype(jnp.float32) / jnp.sqrt(back_squares / COLS + NORM_EPS)
    factor_bf = new_factor.astype(jnp.bfloat16)
    update_full = lax.dot_general(
        left_bf, factor_bf, (((1,), (1,)), ((), ())), preferred_element_type=jnp.float32
    )
    weight_update = (update_full * math.sqrt(ROWS / RANK)).astype(jnp.bfloat16)
    return (new_momentum, weight_update, new_factor)


def solution(mesh):
    placed = (P("row", "col"), P("row", "col"), P("col", None))
    return jax.shard_map(
        local,
        mesh=mesh,
        in_specs=placed,
        out_specs=(P("row", "col"), P("row", "col"), P("col", None)),
        check_vma=False,
    )
```

```python
import math

import jax
import jax.numpy as jnp
from jax import lax
from jax.experimental import pallas as pl
from jax.experimental.pallas import tpu as pltpu
from jax.sharding import PartitionSpec as P

ROWS = 8192
COLS = 26624
RANK = 512


NORM_EPS = 1e-06
GRAM_JITTER = 0.0001
FEEDBACK = 0.25

HIGHEST = lax.Precision.HIGHEST
BLOCK = 128
BLOCKS = RANK // BLOCK
SUB = 8
GROUPS = BLOCK // SUB
PAIRS = [(i, j) for i in range(BLOCKS) for j in range(i, BLOCKS)]


def sub_row(x, k):
    return jnp.broadcast_to(x[k : k + 1, :], (SUB, BLOCK))


def lane_col(x, c):
    return jnp.broadcast_to(x[:, c : c + 1], (SUB, BLOCK))


def pieces(x):
    hi = x.astype(jnp.bfloat16)
    rest = x - hi.astype(jnp.float32)
    mid = rest.astype(jnp.bfloat16)
    return hi, mid, (rest - mid.astype(jnp.float32)).astype(jnp.bfloat16)


def stacked(*parts):
    return jnp.concatenate([x.astype(jnp.float32) for x in parts], axis=0).astype(jnp.bfloat16)


def factor_block(rows):
    sub = lax.broadcasted_iota(jnp.int32, (SUB, BLOCK), 0)
    lane = lax.broadcasted_iota(jnp.int32, (SUB, BLOCK), 1)
    out = []
    for p in range(GROUPS):
        panel = (lane >= SUB * p) & (lane < SUB * (p + 1))
        cols = [lane_col(rows[p], SUB * p + j) for j in range(SUB)]
        x = jnp.where(panel, jnp.where(lane == sub + SUB * p, 1.0, 0.0), rows[p])
        pivots, recips, row_k, upper = [], [], [], []
        for k in range(SUB):
            pivot = sub_row(cols[k], k)
            r = pl.reciprocal(pivot, approx=True)
            m = jnp.where(sub > k, cols[k] * r, 0.0)
            u = {j: sub_row(cols[j], k) for j in range(k + 1, SUB)}
            for j in range(k + 1, SUB):
                cols[j] = cols[j] - m * u[j]
            xk = sub_row(x, k)
            if k < SUB - 1:
                x = x - m * xk
            pivots.append(pivot)
            recips.append(r)
            row_k.append(xk)
            upper.append(u)
        d8 = pivots[0]
        for k in range(1, SUB):
            d8 = jnp.where(sub == k, pivots[k], d8)
        out.append(jnp.where(lane < SUB * (p + 1), x * lax.rsqrt(d8), 0.0))
        if p + 1 < GROUPS:
            b = [lane_col(rows[p + 1], SUB * p + j) for j in range(SUB)]
            y = jnp.where(panel, 0.0, rows[p + 1])
            for k in range(SUB):
                m = b[k] * recips[k]
                for j in range(k + 1, SUB):
                    b[j] = b[j] - m * upper[k][j]
                y = y - m * row_k[k]
            rows[p + 1] = y
        if p + 2 < GROUPS:
            r8 = recips[0]
            for k in range(1, SUB):
                r8 = jnp.where(sub == k, recips[k], r8)
            hi, mid, low = pieces(x)
            hi2, mid2, low2 = pieces(x * r8)
            product = lax.dot_general(
                stacked(hi, hi, mid, mid, hi, low),
                stacked(hi2, mid2, hi2, mid2, low2, hi2),
                (((0,), (0,)), ((), ())),
                preferred_element_type=jnp.float32,
            )
            for q in range(p + 2, GROUPS):
                rows[q] = jnp.where(panel, 0.0, rows[q]) - product[SUB * q : SUB * (q + 1), :]
    return out


def inverse_factor_kernel(g_ref, m_ref, s_ref, d_ref, x_ref, y_ref):
    eye = (
        lax.broadcasted_iota(jnp.int32, (BLOCK, BLOCK), 0)
        == lax.broadcasted_iota(jnp.int32, (BLOCK, BLOCK), 1)
    )
    diagonal = jnp.zeros((BLOCK, BLOCK), jnp.float32)
    for n, (i, j) in enumerate(PAIRS):
        if i == j:
            diagonal += jnp.where(eye, g_ref[n], 0.0)
    jitter = (GRAM_JITTER / RANK) * jnp.sum(diagonal)
    s_ref[...] = jnp.zeros_like(s_ref)
    for n, (i, j) in enumerate(PAIRS):
        x = g_ref[n]
        if i == j:
            x = x + jnp.where(eye, jitter, 0.0)
        s_ref[BLOCK * i : BLOCK * (i + 1), BLOCK * j : BLOCK * (j + 1)] = x

    def block(b, carry):
        lo = pl.multiple_of(b * BLOCK, BLOCK)
        rows = [s_ref[pl.ds(lo + SUB * q, SUB), pl.ds(lo, BLOCK)] for q in range(GROUPS)]
        for q, x in enumerate(factor_block(rows)):
            d_ref[SUB * q : SUB * (q + 1), :] = x
        m_bb = d_ref[...]
        hi, mid, low = pieces(m_bb)
        first = jnp.concatenate([hi, hi, mid, mid, hi, low], axis=1)
        hi, mid, low = pieces(s_ref[pl.ds(lo, BLOCK), :])
        second = jnp.concatenate([hi, mid, hi, mid, low, hi], axis=0)
        s_ref[pl.ds(lo, BLOCK), :] = jnp.dot(first, second, preferred_element_type=jnp.float32)
        s_ref[pl.ds(lo, BLOCK), pl.ds(lo, BLOCK)] = m_bb
        hi, mid, low = pieces(s_ref[pl.ds(lo, BLOCK), :])
        for n, (x, y) in enumerate(((hi, hi), (hi, mid), (mid, hi), (mid, mid), (hi, low), (low, hi))):
            x_ref[BLOCK * n : BLOCK * (n + 1), :] = x
            y_ref[BLOCK * n : BLOCK * (n + 1), :] = y
        for i in range(1, BLOCKS):

            @pl.when(i > b)
            def _():
                here = slice(BLOCK * i, BLOCK * (i + 1))
                s_ref[here, pl.ds(lo, BLOCK)] = jnp.zeros((BLOCK, BLOCK), jnp.float32)
                s_ref[here, :] -= lax.dot_general(
                    x_ref[:, here], y_ref[...], (((0,), (0,)), ((), ())), preferred_element_type=jnp.float32
                )

        return carry

    lax.fori_loop(0, BLOCKS, block, 0)
    for i in range(BLOCKS):
        for j in range(BLOCKS):
            here = (slice(BLOCK * i, BLOCK * (i + 1)), slice(BLOCK * j, BLOCK * (j + 1)))
            m_ref[here] = s_ref[here] if j <= i else jnp.zeros((BLOCK, BLOCK), jnp.float32)


def gram_kernel(p_ref, o_ref):
    for i in range(BLOCKS):
        rows = lax.dot_general(
            p_ref[:, BLOCK * i : BLOCK * (i + 1)],
            p_ref[:, BLOCK * i :],
            (((0,), (0,)), ((), ())),
            precision=HIGHEST,
            preferred_element_type=jnp.float32,
        )
        for j in range(i, BLOCKS):
            o_ref[PAIRS.index((i, j))] = rows[:, BLOCK * (j - i) : BLOCK * (j - i + 1)]


def gram_blocks(projected):
    return pl.pallas_call(
        gram_kernel,
        out_shape=jax.ShapeDtypeStruct((len(PAIRS), BLOCK, BLOCK), jnp.float32),
        in_specs=[pl.BlockSpec(memory_space=pltpu.VMEM)],
        out_specs=pl.BlockSpec(memory_space=pltpu.VMEM),
        compiler_params=pltpu.CompilerParams(vmem_limit_bytes=16 * 1024 * 1024),
        cost_estimate=pl.CostEstimate(flops=2**31, bytes_accessed=2**21, transcendentals=0),
    )(projected)


def inverse_factor(blocks):
    return pl.pallas_call(
        inverse_factor_kernel,
        out_shape=jax.ShapeDtypeStruct((RANK, RANK), jnp.float32),
        in_specs=[pl.BlockSpec(memory_space=pltpu.VMEM)],
        out_specs=pl.BlockSpec(memory_space=pltpu.VMEM),
        scratch_shapes=[
            pltpu.VMEM((RANK, RANK), jnp.float32),
            pltpu.VMEM((BLOCK, BLOCK), jnp.float32),
            pltpu.VMEM((6 * BLOCK, RANK), jnp.bfloat16),
            pltpu.VMEM((6 * BLOCK, RANK), jnp.bfloat16),
        ],
        compiler_params=pltpu.CompilerParams(vmem_limit_bytes=16 * 1024 * 1024),
        cost_estimate=pl.CostEstimate(flops=26 * 10**9, bytes_accessed=2**21, transcendentals=0),
    )(blocks)


def weights_kernel(half_ref, b_ref, p_ref, *refs):
    *added, o_ref, w_ref, buf_ref, sems = refs
    half = half_ref[0]
    width = buf_ref.shape[1]
    start = b_ref.shape[1] - width
    cut = (width // BLOCK + 1) // 2 * BLOCK
    chunks = (pl.ds(0, cut), pl.ds(cut, width - cut))
    copies = [
        pltpu.make_async_copy(
            b_ref.at[:, pl.ds(pl.multiple_of(half * start + chunk.start, BLOCK), chunk.size)],
            buf_ref.at[:, chunk],
            sems.at[n],
        )
        for n, chunk in enumerate(chunks)
    ]
    for copy in copies:
        copy.start()
    parts = pieces(p_ref[...])
    for copy, chunk in zip(copies, chunks):
        copy.wait()
        for n, piece in enumerate(parts):
            term = lax.dot_general(
                buf_ref[:, chunk], piece, (((0,), (0,)), ((), ())), preferred_element_type=jnp.float32
            )
            w_ref[chunk, :] = term if n == 0 else w_ref[chunk, :] + term
    own = w_ref[pl.ds(pl.multiple_of(half * (o_ref.shape[0] - start), SUB), o_ref.shape[0]), :]
    o_ref[...] = own + added[0][...] if added else own


def weights_half(half, blended, projected, *added):
    rows = blended.shape[1] // 2
    width = blended.shape[1] - rows // BLOCK * BLOCK
    vmem = pl.BlockSpec(memory_space=pltpu.VMEM)
    return pl.pallas_call(
        weights_kernel,
        out_shape=jax.ShapeDtypeStruct((rows, RANK), jnp.float32),
        in_specs=[
            pl.BlockSpec(memory_space=pltpu.SMEM),
            pl.BlockSpec(memory_space=pl.ANY),
            vmem,
        ]
        + [vmem] * len(added),
        out_specs=vmem,
        scratch_shapes=[
            pltpu.VMEM((width, RANK), jnp.float32),
            pltpu.VMEM((blended.shape[0], width), jnp.bfloat16),
            pltpu.SemaphoreType.DMA((2,)),
        ],
        compiler_params=pltpu.CompilerParams(vmem_limit_bytes=60 * 1024 * 1024),
        cost_estimate=pl.CostEstimate(flops=2**28, bytes_accessed=2**20, transcendentals=0),
    )(half.astype(jnp.int32).reshape(1), blended, projected, *added)


def scatter_sum(x, axis, size):
    parts = x.reshape((size, x.shape[0] // size) + x.shape[1:])
    return jnp.sum(lax.all_to_all(parts, axis, 0, 0), axis=0)


def exchange(x, axis, groups, size):
    return lax.all_to_all(jnp.broadcast_to(x, (size,) + x.shape), axis, 0, 0, axis_index_groups=groups)


def local(momentum, gradient, right_factor):
    n_col = lax.axis_size("col")
    n_row = lax.axis_size("row")
    n_z = n_row // 2
    core = lax.axis_index("row") % 2
    other = [(i, i ^ 1) for i in range(n_row)]
    along_z = [[2 * z + c for z in range(n_z)] for c in range(2)]

    def both_halves(mine):
        theirs = lax.ppermute(mine, "row", other)
        return jnp.concatenate([jnp.where(core == 0, mine, theirs), jnp.where(core == 0, theirs, mine)])

    blended = (momentum.astype(jnp.float32) + gradient.astype(jnp.float32)).astype(jnp.bfloat16)
    partial_proj = jnp.dot(blended, right_factor, preferred_element_type=jnp.float32)
    projected = exchange(scatter_sum(partial_proj, "col", n_col), "col", None, n_col).reshape(partial_proj.shape)

    packed = gram_blocks(projected).reshape(len(PAIRS) * BLOCK, BLOCK)
    share = packed.shape[0] // n_col
    packed = lax.dynamic_slice_in_dim(packed, lax.axis_index("col") * share, share, 0)
    packed = packed + lax.ppermute(packed, "row", other)
    packed, projected = lax.optimization_barrier((packed, projected))
    packed = jnp.sum(exchange(packed, "row", along_z, n_z), axis=0)
    packed = exchange(packed, "col", None, n_col).reshape(len(PAIRS), BLOCK, BLOCK)

    theirs = lax.ppermute(weights_half(1 - core, blended, projected), "row", other)
    weights = weights_half(core, blended, projected, theirs)
    weights = lax.psum_scatter(
        weights, "row", scatter_dimension=0, axis_index_groups=along_z, tiled=True
    )

    inverse = inverse_factor(packed)
    back_rows = jnp.dot(weights, inverse.T, precision=HIGHEST, preferred_element_type=jnp.float32)
    half = lax.all_gather(
        back_rows.astype(jnp.bfloat16), "row", axis_index_groups=along_z, tiled=True
    )
    squares = jnp.sum(jnp.square(half.astype(jnp.float32)), axis=0).reshape(BLOCKS, BLOCK)
    squares = squares + lax.ppermute(squares, "row", other)
    squares, projected, inverse = lax.optimization_barrier((squares, projected, inverse))
    squares = exchange(squares, "col", None, n_col)
    right_bf = both_halves(half)
    left_bf = jnp.dot(
        projected, inverse.T, precision=HIGHEST, preferred_element_type=jnp.float32
    ).astype(jnp.bfloat16)
    correction = lax.dot_general(
        left_bf, right_bf, (((1,), (1,)), ((), ())), preferred_element_type=jnp.float32
    )
    new_momentum = (blended.astype(jnp.float32) - FEEDBACK * correction).astype(jnp.bfloat16)
    squares, new_momentum = lax.optimization_barrier((squares, new_momentum))
    back_squares = jnp.sum(squares, axis=0).reshape(RANK)
    new_factor = right_bf.astype(jnp.float32) * (1.0 / jnp.sqrt(back_squares / COLS + NORM_EPS))
    factor_bf = new_factor.astype(jnp.bfloat16)
    update_full = lax.dot_general(
        left_bf, factor_bf, (((1,), (1,)), ((), ())), preferred_element_type=jnp.float32
    )
    weight_update = (update_full * math.sqrt(ROWS / RANK)).astype(jnp.bfloat16)
    return (new_momentum, weight_update, new_factor)


def solution(mesh):
    placed = (P("row", "col"), P("row", "col"), P("col", None))
    return jax.shard_map(
        local,
        mesh=mesh,
        in_specs=placed,
        out_specs=(P("row", "col"), P("row", "col"), P("col", None)),
        check_vma=False,
    )
```

```python
import math

import jax
import jax.numpy as jnp
from jax import lax
from jax.experimental import pallas as pl
from jax.experimental.pallas import tpu as pltpu
from jax.sharding import PartitionSpec as P

ROWS = 8192
COLS = 26624
RANK = 512


NORM_EPS = 1e-06
GRAM_JITTER = 0.0001
FEEDBACK = 0.25

HIGHEST = lax.Precision.HIGHEST
BLOCK = 128
BLOCKS = RANK // BLOCK
SUB = 8
GROUPS = BLOCK // SUB
PAIRS = [(i, j) for i in range(BLOCKS) for j in range(i, BLOCKS)]


def sub_row(x, k):
    return jnp.broadcast_to(x[k : k + 1, :], (SUB, BLOCK))


def lane_col(x, c):
    return jnp.broadcast_to(x[:, c : c + 1], (SUB, BLOCK))


def pieces(x):
    hi = x.astype(jnp.bfloat16)
    rest = x - hi.astype(jnp.float32)
    mid = rest.astype(jnp.bfloat16)
    return hi, mid, (rest - mid.astype(jnp.float32)).astype(jnp.bfloat16)


def stacked(*parts):
    return jnp.concatenate([x.astype(jnp.float32) for x in parts], axis=0).astype(jnp.bfloat16)


def factor_block(rows):
    sub = lax.broadcasted_iota(jnp.int32, (SUB, BLOCK), 0)
    lane = lax.broadcasted_iota(jnp.int32, (SUB, BLOCK), 1)
    out = []
    for p in range(GROUPS):
        panel = (lane >= SUB * p) & (lane < SUB * (p + 1))
        cols = [lane_col(rows[p], SUB * p + j) for j in range(SUB)]
        x = jnp.where(panel, jnp.where(lane == sub + SUB * p, 1.0, 0.0), rows[p])
        pivots, recips, row_k, upper = [], [], [], []
        for k in range(SUB):
            pivot = sub_row(cols[k], k)
            r = pl.reciprocal(pivot, approx=True)
            m = jnp.where(sub > k, cols[k] * r, 0.0)
            u = {j: sub_row(cols[j], k) for j in range(k + 1, SUB)}
            for j in range(k + 1, SUB):
                cols[j] = cols[j] - m * u[j]
            xk = sub_row(x, k)
            if k < SUB - 1:
                x = x - m * xk
            pivots.append(pivot)
            recips.append(r)
            row_k.append(xk)
            upper.append(u)
        d8 = pivots[0]
        for k in range(1, SUB):
            d8 = jnp.where(sub == k, pivots[k], d8)
        out.append(jnp.where(lane < SUB * (p + 1), x * lax.rsqrt(d8), 0.0))
        if p + 1 < GROUPS:
            b = [lane_col(rows[p + 1], SUB * p + j) for j in range(SUB)]
            y = jnp.where(panel, 0.0, rows[p + 1])
            for k in range(SUB):
                m = b[k] * recips[k]
                for j in range(k + 1, SUB):
                    b[j] = b[j] - m * upper[k][j]
                y = y - m * row_k[k]
            rows[p + 1] = y
        if p + 2 < GROUPS:
            r8 = recips[0]
            for k in range(1, SUB):
                r8 = jnp.where(sub == k, recips[k], r8)
            hi, mid, low = pieces(x)
            hi2, mid2, low2 = pieces(x * r8)
            product = lax.dot_general(
                stacked(hi, hi, mid, mid, hi, low),
                stacked(hi2, mid2, hi2, mid2, low2, hi2),
                (((0,), (0,)), ((), ())),
                preferred_element_type=jnp.float32,
            )
            for q in range(p + 2, GROUPS):
                rows[q] = jnp.where(panel, 0.0, rows[q]) - product[SUB * q : SUB * (q + 1), :]
    return out


def inverse_factor_kernel(core_ref, mine_ref, theirs_ref, m_ref, s_ref, d_ref, x_ref, y_ref):
    half = mine_ref.shape[0]

    def gram(n):
        return jnp.where(core_ref[0] == n // half, mine_ref[n % half], theirs_ref[n % half])

    eye = (
        lax.broadcasted_iota(jnp.int32, (BLOCK, BLOCK), 0)
        == lax.broadcasted_iota(jnp.int32, (BLOCK, BLOCK), 1)
    )
    diagonal = jnp.zeros((BLOCK, BLOCK), jnp.float32)
    for n, (i, j) in enumerate(PAIRS):
        if i == j:
            diagonal += jnp.where(eye, gram(n), 0.0)
    jitter = (GRAM_JITTER / RANK) * jnp.sum(diagonal)
    s_ref[...] = jnp.zeros_like(s_ref)
    for n, (i, j) in enumerate(PAIRS):
        x = gram(n)
        if i == j:
            x = x + jnp.where(eye, jitter, 0.0)
        s_ref[BLOCK * i : BLOCK * (i + 1), BLOCK * j : BLOCK * (j + 1)] = x

    def block(b, carry):
        lo = pl.multiple_of(b * BLOCK, BLOCK)
        rows = [s_ref[pl.ds(lo + SUB * q, SUB), pl.ds(lo, BLOCK)] for q in range(GROUPS)]
        for q, x in enumerate(factor_block(rows)):
            d_ref[SUB * q : SUB * (q + 1), :] = x
        m_bb = d_ref[...]
        hi, mid, low = pieces(m_bb)
        first = jnp.concatenate([hi, hi, mid, mid, hi, low], axis=1)
        hi, mid, low = pieces(s_ref[pl.ds(lo, BLOCK), :])
        second = jnp.concatenate([hi, mid, hi, mid, low, hi], axis=0)
        s_ref[pl.ds(lo, BLOCK), :] = jnp.dot(first, second, preferred_element_type=jnp.float32)
        s_ref[pl.ds(lo, BLOCK), pl.ds(lo, BLOCK)] = m_bb
        hi, mid, low = pieces(s_ref[pl.ds(lo, BLOCK), :])
        for n, (x, y) in enumerate(((hi, hi), (hi, mid), (mid, hi), (mid, mid), (hi, low), (low, hi))):
            x_ref[BLOCK * n : BLOCK * (n + 1), :] = x
            y_ref[BLOCK * n : BLOCK * (n + 1), :] = y
        for i in range(1, BLOCKS):

            @pl.when(i > b)
            def _():
                here = slice(BLOCK * i, BLOCK * (i + 1))
                s_ref[here, pl.ds(lo, BLOCK)] = jnp.zeros((BLOCK, BLOCK), jnp.float32)
                s_ref[here, :] -= lax.dot_general(
                    x_ref[:, here], y_ref[...], (((0,), (0,)), ((), ())), preferred_element_type=jnp.float32
                )

        return carry

    lax.fori_loop(0, BLOCKS, block, 0)
    for i in range(BLOCKS):
        for j in range(BLOCKS):
            here = (slice(BLOCK * i, BLOCK * (i + 1)), slice(BLOCK * j, BLOCK * (j + 1)))
            m_ref[here] = s_ref[here] if j <= i else jnp.zeros((BLOCK, BLOCK), jnp.float32)


def gram_kernel(p_ref, o_ref):
    for i in range(BLOCKS):
        rows = lax.dot_general(
            p_ref[:, BLOCK * i : BLOCK * (i + 1)],
            p_ref[:, BLOCK * i :],
            (((0,), (0,)), ((), ())),
            precision=HIGHEST,
            preferred_element_type=jnp.float32,
        )
        for j in range(i, BLOCKS):
            o_ref[PAIRS.index((i, j))] = rows[:, BLOCK * (j - i) : BLOCK * (j - i + 1)]


def gram_blocks(projected):
    return pl.pallas_call(
        gram_kernel,
        out_shape=jax.ShapeDtypeStruct((len(PAIRS), BLOCK, BLOCK), jnp.float32),
        in_specs=[pl.BlockSpec(memory_space=pltpu.VMEM)],
        out_specs=pl.BlockSpec(memory_space=pltpu.VMEM),
        compiler_params=pltpu.CompilerParams(vmem_limit_bytes=16 * 1024 * 1024),
        cost_estimate=pl.CostEstimate(flops=2**31, bytes_accessed=2**21, transcendentals=0),
    )(projected)


def inverse_factor(core, mine, theirs):
    return pl.pallas_call(
        inverse_factor_kernel,
        out_shape=jax.ShapeDtypeStruct((RANK, RANK), jnp.float32),
        in_specs=[pl.BlockSpec(memory_space=pltpu.SMEM)] + [pl.BlockSpec(memory_space=pltpu.VMEM)] * 2,
        out_specs=pl.BlockSpec(memory_space=pltpu.VMEM),
        scratch_shapes=[
            pltpu.VMEM((RANK, RANK), jnp.float32),
            pltpu.VMEM((BLOCK, BLOCK), jnp.float32),
            pltpu.VMEM((6 * BLOCK, RANK), jnp.bfloat16),
            pltpu.VMEM((6 * BLOCK, RANK), jnp.bfloat16),
        ],
        compiler_params=pltpu.CompilerParams(vmem_limit_bytes=16 * 1024 * 1024),
        cost_estimate=pl.CostEstimate(flops=29 * 10**9, bytes_accessed=2**21, transcendentals=0),
    )(core.astype(jnp.int32).reshape(1), mine, theirs)


def weights_kernel(half_ref, b_ref, p_ref, *refs):
    *added, o_ref, w_ref = refs
    start = b_ref.shape[1] - w_ref.shape[0]
    half = half_ref[0]
    rows = b_ref[:, pl.ds(pl.multiple_of(half * start, BLOCK), w_ref.shape[0])]
    for n, piece in enumerate(pieces(p_ref[...])):
        term = lax.dot_general(rows, piece, (((0,), (0,)), ((), ())), preferred_element_type=jnp.float32)
        w_ref[...] = term if n == 0 else w_ref[...] + term
    own = w_ref[pl.ds(pl.multiple_of(half * (o_ref.shape[0] - start), SUB), o_ref.shape[0]), :]
    o_ref[...] = own + added[0][...] if added else own


def weights_half(half, blended, projected, *added):
    rows = blended.shape[1] // 2
    start = rows // BLOCK * BLOCK
    vmem = pl.BlockSpec(memory_space=pltpu.VMEM)
    return pl.pallas_call(
        weights_kernel,
        out_shape=jax.ShapeDtypeStruct((rows, RANK), jnp.float32),
        in_specs=[pl.BlockSpec(memory_space=pltpu.SMEM)] + [vmem] * (2 + len(added)),
        out_specs=vmem,
        scratch_shapes=[pltpu.VMEM((blended.shape[1] - start, RANK), jnp.float32)],
        compiler_params=pltpu.CompilerParams(vmem_limit_bytes=32 * 1024 * 1024),
        cost_estimate=pl.CostEstimate(flops=2**31, bytes_accessed=2**22, transcendentals=0),
    )(half.astype(jnp.int32).reshape(1), blended, projected, *added)


def scatter_sum(x, axis, size):
    parts = x.reshape((size, x.shape[0] // size) + x.shape[1:])
    return jnp.sum(lax.all_to_all(parts, axis, 0, 0), axis=0)


def exchange(x, axis, groups, size):
    return lax.all_to_all(jnp.broadcast_to(x, (size,) + x.shape), axis, 0, 0, axis_index_groups=groups)


def local(momentum, gradient, right_factor):
    n_col = lax.axis_size("col")
    n_row = lax.axis_size("row")
    n_z = n_row // 2
    core = lax.axis_index("row") % 2
    other = [(i, i ^ 1) for i in range(n_row)]
    along_z = [[2 * z + c for z in range(n_z)] for c in range(2)]

    def both_halves(mine):
        theirs = lax.ppermute(mine, "row", other)
        return jnp.concatenate([jnp.where(core == 0, mine, theirs), jnp.where(core == 0, theirs, mine)])

    blended = (momentum.astype(jnp.float32) + gradient.astype(jnp.float32)).astype(jnp.bfloat16)
    partial_proj = jnp.dot(blended, right_factor, preferred_element_type=jnp.float32)
    projected = exchange(scatter_sum(partial_proj, "col", n_col), "col", None, n_col).reshape(partial_proj.shape)

    theirs = weights_half(1 - core, blended, projected)
    theirs, projected = lax.optimization_barrier((theirs, projected))
    theirs = lax.ppermute(theirs, "row", other)

    packed = gram_blocks(projected).reshape(2, len(PAIRS) // 2 * BLOCK, BLOCK)
    share = packed.shape[1] // n_col
    here = lax.axis_index("col") * share
    mine, for_other = (
        lax.dynamic_slice(packed, (which, here, 0), (1, share, BLOCK))[0] for which in (core, 1 - core)
    )
    packed = mine + lax.ppermute(for_other, "row", other)

    weights = weights_half(core, blended, projected, theirs)
    weights = lax.psum_scatter(
        weights, "row", scatter_dimension=0, axis_index_groups=along_z, tiled=True
    )
    packed = jnp.sum(exchange(packed, "row", along_z, n_z), axis=0)
    packed = exchange(packed, "col", None, n_col).reshape(len(PAIRS) // 2, BLOCK, BLOCK)

    inverse = inverse_factor(core, packed, lax.ppermute(packed, "row", other))
    back_rows = jnp.dot(weights, inverse.T, precision=HIGHEST, preferred_element_type=jnp.float32)
    half = lax.all_gather(
        back_rows.astype(jnp.bfloat16), "row", axis_index_groups=along_z, tiled=True
    )
    squares = jnp.sum(jnp.square(half.astype(jnp.float32)), axis=0).reshape(BLOCKS, BLOCK)
    squares = squares + lax.ppermute(squares, "row", other)
    squares, projected, inverse = lax.optimization_barrier((squares, projected, inverse))
    squares = exchange(squares, "col", None, n_col)
    right_bf = both_halves(half)
    left_bf = jnp.dot(
        projected, inverse.T, precision=HIGHEST, preferred_element_type=jnp.float32
    ).astype(jnp.bfloat16)
    correction = lax.dot_general(
        left_bf, right_bf, (((1,), (1,)), ((), ())), preferred_element_type=jnp.float32
    )
    new_momentum = (blended.astype(jnp.float32) - FEEDBACK * correction).astype(jnp.bfloat16)
    squares, new_momentum = lax.optimization_barrier((squares, new_momentum))
    back_squares = jnp.sum(squares, axis=0).reshape(RANK)
    new_factor = right_bf.astype(jnp.float32) * (1.0 / jnp.sqrt(back_squares / COLS + NORM_EPS))
    factor_bf = new_factor.astype(jnp.bfloat16)
    update_full = lax.dot_general(
        left_bf, factor_bf, (((1,), (1,)), ((), ())), preferred_element_type=jnp.float32
    )
    weight_update = (update_full * math.sqrt(ROWS / RANK)).astype(jnp.bfloat16)
    return (new_momentum, weight_update, new_factor)


def solution(mesh):
    placed = (P("row", "col"), P("row", "col"), P("col", None))
    return jax.shard_map(
        local,
        mesh=mesh,
        in_specs=placed,
        out_specs=(P("row", "col"), P("row", "col"), P("col", None)),
        check_vma=False,
    )
```

```python
import math

import jax
import jax.numpy as jnp
from jax import lax
from jax.experimental import pallas as pl
from jax.experimental.pallas import tpu as pltpu
from jax.sharding import PartitionSpec as P

ROWS = 8192
COLS = 26624
RANK = 512


NORM_EPS = 1e-06
GRAM_JITTER = 0.0001
FEEDBACK = 0.25

HIGHEST = lax.Precision.HIGHEST
BLOCK = 128
BLOCKS = RANK // BLOCK
SUB = 8
GROUPS = BLOCK // SUB
PAIRS = [(i, j) for i in range(BLOCKS) for j in range(i, BLOCKS)]


def sub_row(x, k):
    return jnp.broadcast_to(x[k : k + 1, :], (SUB, BLOCK))


def lane_col(x, c):
    return jnp.broadcast_to(x[:, c : c + 1], (SUB, BLOCK))


def pieces(x):
    hi = x.astype(jnp.bfloat16)
    rest = x - hi.astype(jnp.float32)
    mid = rest.astype(jnp.bfloat16)
    return hi, mid, (rest - mid.astype(jnp.float32)).astype(jnp.bfloat16)


def stacked(*parts):
    return jnp.concatenate([x.astype(jnp.float32) for x in parts], axis=0).astype(jnp.bfloat16)


def factor_block(rows):
    sub = lax.broadcasted_iota(jnp.int32, (SUB, BLOCK), 0)
    lane = lax.broadcasted_iota(jnp.int32, (SUB, BLOCK), 1)
    out = []
    for p in range(GROUPS):
        panel = (lane >= SUB * p) & (lane < SUB * (p + 1))
        cols = [lane_col(rows[p], SUB * p + j) for j in range(SUB)]
        x = jnp.where(panel, jnp.where(lane == sub + SUB * p, 1.0, 0.0), rows[p])
        pivots, recips, row_k, upper = [], [], [], []
        for k in range(SUB):
            pivot = sub_row(cols[k], k)
            r = pl.reciprocal(pivot, approx=True)
            m = jnp.where(sub > k, cols[k] * r, 0.0)
            u = {j: sub_row(cols[j], k) for j in range(k + 1, SUB)}
            for j in range(k + 1, SUB):
                cols[j] = cols[j] - m * u[j]
            xk = sub_row(x, k)
            if k < SUB - 1:
                x = x - m * xk
            pivots.append(pivot)
            recips.append(r)
            row_k.append(xk)
            upper.append(u)
        d8 = pivots[0]
        for k in range(1, SUB):
            d8 = jnp.where(sub == k, pivots[k], d8)
        out.append(jnp.where(lane < SUB * (p + 1), x * lax.rsqrt(d8), 0.0))
        if p + 1 < GROUPS:
            b = [lane_col(rows[p + 1], SUB * p + j) for j in range(SUB)]
            y = jnp.where(panel, 0.0, rows[p + 1])
            for k in range(SUB):
                m = b[k] * recips[k]
                for j in range(k + 1, SUB):
                    b[j] = b[j] - m * upper[k][j]
                y = y - m * row_k[k]
            rows[p + 1] = y
        if p + 2 < GROUPS:
            r8 = recips[0]
            for k in range(1, SUB):
                r8 = jnp.where(sub == k, recips[k], r8)
            hi, mid, low = pieces(x)
            hi2, mid2, low2 = pieces(x * r8)
            product = lax.dot_general(
                stacked(hi, hi, mid, mid, hi, low),
                stacked(hi2, mid2, hi2, mid2, low2, hi2),
                (((0,), (0,)), ((), ())),
                preferred_element_type=jnp.float32,
            )
            for q in range(p + 2, GROUPS):
                rows[q] = jnp.where(panel, 0.0, rows[q]) - product[SUB * q : SUB * (q + 1), :]
    return out


def inverse_factor_kernel(core_ref, mine_ref, theirs_ref, m_ref, s_ref, d_ref, x_ref, y_ref):
    half = mine_ref.shape[0]

    def gram(n):
        return jnp.where(core_ref[0] == n // half, mine_ref[n % half], theirs_ref[n % half])

    eye = (
        lax.broadcasted_iota(jnp.int32, (BLOCK, BLOCK), 0)
        == lax.broadcasted_iota(jnp.int32, (BLOCK, BLOCK), 1)
    )
    diagonal = jnp.zeros((BLOCK, BLOCK), jnp.float32)
    for n, (i, j) in enumerate(PAIRS):
        if i == j:
            diagonal += jnp.where(eye, gram(n), 0.0)
    jitter = (GRAM_JITTER / RANK) * jnp.sum(diagonal)
    s_ref[...] = jnp.zeros_like(s_ref)
    for n, (i, j) in enumerate(PAIRS):
        x = gram(n)
        if i == j:
            x = x + jnp.where(eye, jitter, 0.0)
        s_ref[BLOCK * i : BLOCK * (i + 1), BLOCK * j : BLOCK * (j + 1)] = x

    def block(b, carry):
        lo = pl.multiple_of(b * BLOCK, BLOCK)
        rows = [s_ref[pl.ds(lo + SUB * q, SUB), pl.ds(lo, BLOCK)] for q in range(GROUPS)]
        for q, x in enumerate(factor_block(rows)):
            d_ref[SUB * q : SUB * (q + 1), :] = x
        m_bb = d_ref[...]
        hi, mid, low = pieces(m_bb)
        first = jnp.concatenate([hi, hi, mid, mid, hi, low], axis=1)
        hi, mid, low = pieces(s_ref[pl.ds(lo, BLOCK), :])
        second = jnp.concatenate([hi, mid, hi, mid, low, hi], axis=0)
        s_ref[pl.ds(lo, BLOCK), :] = jnp.dot(first, second, preferred_element_type=jnp.float32)
        s_ref[pl.ds(lo, BLOCK), pl.ds(lo, BLOCK)] = m_bb
        hi, mid, low = pieces(s_ref[pl.ds(lo, BLOCK), :])
        for n, (x, y) in enumerate(((hi, hi), (hi, mid), (mid, hi), (mid, mid), (hi, low), (low, hi))):
            x_ref[BLOCK * n : BLOCK * (n + 1), :] = x
            y_ref[BLOCK * n : BLOCK * (n + 1), :] = y
        for i in range(1, BLOCKS):

            @pl.when(i > b)
            def _():
                here = slice(BLOCK * i, BLOCK * (i + 1))
                s_ref[here, pl.ds(lo, BLOCK)] = jnp.zeros((BLOCK, BLOCK), jnp.float32)
                s_ref[here, :] -= lax.dot_general(
                    x_ref[:, here], y_ref[...], (((0,), (0,)), ((), ())), preferred_element_type=jnp.float32
                )

        return carry

    lax.fori_loop(0, BLOCKS, block, 0)
    for i in range(BLOCKS):
        for j in range(BLOCKS):
            here = (slice(BLOCK * i, BLOCK * (i + 1)), slice(BLOCK * j, BLOCK * (j + 1)))
            m_ref[here] = s_ref[here] if j <= i else jnp.zeros((BLOCK, BLOCK), jnp.float32)


def gram_kernel(p_ref, o_ref):
    for i in range(BLOCKS):
        rows = lax.dot_general(
            p_ref[:, BLOCK * i : BLOCK * (i + 1)],
            p_ref[:, BLOCK * i :],
            (((0,), (0,)), ((), ())),
            precision=HIGHEST,
            preferred_element_type=jnp.float32,
        )
        for j in range(i, BLOCKS):
            o_ref[PAIRS.index((i, j))] = rows[:, BLOCK * (j - i) : BLOCK * (j - i + 1)]


def gram_blocks(projected):
    return pl.pallas_call(
        gram_kernel,
        out_shape=jax.ShapeDtypeStruct((len(PAIRS), BLOCK, BLOCK), jnp.float32),
        in_specs=[pl.BlockSpec(memory_space=pltpu.VMEM)],
        out_specs=pl.BlockSpec(memory_space=pltpu.VMEM),
        compiler_params=pltpu.CompilerParams(vmem_limit_bytes=16 * 1024 * 1024),
        cost_estimate=pl.CostEstimate(flops=2**31, bytes_accessed=2**21, transcendentals=0),
    )(projected)


def inverse_factor(core, mine, theirs):
    return pl.pallas_call(
        inverse_factor_kernel,
        out_shape=jax.ShapeDtypeStruct((RANK, RANK), jnp.float32),
        in_specs=[pl.BlockSpec(memory_space=pltpu.SMEM)] + [pl.BlockSpec(memory_space=pltpu.VMEM)] * 2,
        out_specs=pl.BlockSpec(memory_space=pltpu.VMEM),
        scratch_shapes=[
            pltpu.VMEM((RANK, RANK), jnp.float32),
            pltpu.VMEM((BLOCK, BLOCK), jnp.float32),
            pltpu.VMEM((6 * BLOCK, RANK), jnp.bfloat16),
            pltpu.VMEM((6 * BLOCK, RANK), jnp.bfloat16),
        ],
        compiler_params=pltpu.CompilerParams(vmem_limit_bytes=16 * 1024 * 1024),
        cost_estimate=pl.CostEstimate(flops=29 * 10**9, bytes_accessed=2**21, transcendentals=0),
    )(core.astype(jnp.int32).reshape(1), mine, theirs)


def weights_kernel(core_ref, b_ref, p_ref, mine_ref, theirs_ref, w_ref):
    for n, piece in enumerate(pieces(p_ref[...])):
        term = lax.dot_general(
            b_ref[...], piece, (((0,), (0,)), ((), ())), preferred_element_type=jnp.float32
        )
        w_ref[...] = term if n == 0 else w_ref[...] + term
    half = mine_ref.shape[0]
    core = core_ref[0]
    mine_ref[...] = w_ref[pl.ds(pl.multiple_of(core * half, SUB), half), :]
    theirs_ref[...] = w_ref[pl.ds(pl.multiple_of((1 - core) * half, SUB), half), :]


def weights_halves(core, blended, projected):
    half = jax.ShapeDtypeStruct((blended.shape[1] // 2, RANK), jnp.float32)
    vmem = pl.BlockSpec(memory_space=pltpu.VMEM)
    return pl.pallas_call(
        weights_kernel,
        out_shape=(half, half),
        in_specs=[pl.BlockSpec(memory_space=pltpu.SMEM), vmem, vmem],
        out_specs=(vmem, vmem),
        scratch_shapes=[pltpu.VMEM((blended.shape[1], RANK), jnp.float32)],
        compiler_params=pltpu.CompilerParams(vmem_limit_bytes=32 * 1024 * 1024),
        cost_estimate=pl.CostEstimate(flops=2**32, bytes_accessed=2**22, transcendentals=0),
    )(core.astype(jnp.int32).reshape(1), blended, projected)


def add_kernel(a_ref, b_ref, o_ref):
    o_ref[...] = a_ref[...] + b_ref[...]


def add(a, b, steps):
    block = pl.BlockSpec((a.shape[0] // steps, a.shape[1]), lambda i: (i, 0))
    return pl.pallas_call(
        add_kernel,
        out_shape=jax.ShapeDtypeStruct(a.shape, a.dtype),
        grid=(steps,),
        in_specs=[block, block],
        out_specs=block,
        cost_estimate=pl.CostEstimate(flops=2**19, bytes_accessed=2**22, transcendentals=0),
    )(a, b)


def finish_kernel(scale_ref, right_ref, left_ref, factor_ref, update_ref, f_ref, u_ref, sems):
    total = right_ref.shape[0]
    cut = (total // BLOCK + 1) // 2 * BLOCK
    copies = []
    for chunk in (slice(0, cut), slice(cut, total)):
        f_ref[chunk, :] = right_ref[chunk, :].astype(jnp.float32) * scale_ref[...]
        copies.append(
            pltpu.make_async_copy(f_ref.at[chunk, :], factor_ref.at[chunk, :], sems.at[len(copies)])
        )
        copies[-1].start()
        update = lax.dot_general(
            left_ref[...],
            f_ref[chunk, :].astype(jnp.bfloat16),
            (((1,), (1,)), ((), ())),
            preferred_element_type=jnp.float32,
        )
        u_ref[:, chunk] = (update * math.sqrt(ROWS / RANK)).astype(jnp.bfloat16)
        copies.append(
            pltpu.make_async_copy(u_ref.at[:, chunk], update_ref.at[:, chunk], sems.at[len(copies)])
        )
        copies[-1].start()
    for copy in copies:
        copy.wait()


def finish(scale, right_bf, left_bf):
    factor = jax.ShapeDtypeStruct(right_bf.shape, jnp.float32)
    update = jax.ShapeDtypeStruct((left_bf.shape[0], right_bf.shape[0]), jnp.bfloat16)
    return pl.pallas_call(
        finish_kernel,
        out_shape=(factor, update),
        in_specs=[pl.BlockSpec(memory_space=pltpu.VMEM)] * 3,
        out_specs=(pl.BlockSpec(memory_space=pl.ANY), pl.BlockSpec(memory_space=pl.ANY)),
        scratch_shapes=[
            pltpu.VMEM(factor.shape, factor.dtype),
            pltpu.VMEM(update.shape, update.dtype),
            pltpu.SemaphoreType.DMA((4,)),
        ],
        compiler_params=pltpu.CompilerParams(vmem_limit_bytes=32 * 1024 * 1024),
        cost_estimate=pl.CostEstimate(flops=2**30, bytes_accessed=2**23, transcendentals=0),
    )(scale, right_bf, left_bf)


def scatter_sum(x, axis, size):
    parts = x.reshape((size, x.shape[0] // size) + x.shape[1:])
    return jnp.sum(lax.all_to_all(parts, axis, 0, 0), axis=0)


def exchange(x, axis, groups, size):
    return lax.all_to_all(jnp.broadcast_to(x, (size,) + x.shape), axis, 0, 0, axis_index_groups=groups)


def local(momentum, gradient, right_factor):
    n_col = lax.axis_size("col")
    n_row = lax.axis_size("row")
    n_z = n_row // 2
    core = lax.axis_index("row") % 2
    other = [(i, i ^ 1) for i in range(n_row)]
    along_z = [[2 * z + c for z in range(n_z)] for c in range(2)]

    def both_halves(mine):
        theirs = lax.ppermute(mine, "row", other)
        return jnp.concatenate([jnp.where(core == 0, mine, theirs), jnp.where(core == 0, theirs, mine)])

    blended = (momentum.astype(jnp.float32) + gradient.astype(jnp.float32)).astype(jnp.bfloat16)
    partial_proj = jnp.dot(blended, right_factor, preferred_element_type=jnp.float32)
    projected = exchange(scatter_sum(partial_proj, "col", n_col), "col", None, n_col).reshape(partial_proj.shape)

    ours, theirs = weights_halves(core, blended, projected)
    theirs, projected = lax.optimization_barrier((theirs, projected))
    theirs = lax.ppermute(theirs, "row", other)

    packed = gram_blocks(projected).reshape(2, len(PAIRS) // 2 * BLOCK, BLOCK)
    share = packed.shape[1] // n_col
    here = lax.axis_index("col") * share
    mine, for_other = (
        lax.dynamic_slice(packed, (which, here, 0), (1, share, BLOCK))[0] for which in (core, 1 - core)
    )
    packed = mine + lax.ppermute(for_other, "row", other)

    weights = add(ours, theirs, 4)
    weights = lax.psum_scatter(
        weights, "row", scatter_dimension=0, axis_index_groups=along_z, tiled=True
    )
    packed = jnp.sum(exchange(packed, "row", along_z, n_z), axis=0)
    packed = exchange(packed, "col", None, n_col).reshape(len(PAIRS) // 2, BLOCK, BLOCK)

    inverse = inverse_factor(core, packed, lax.ppermute(packed, "row", other))
    back_rows = jnp.dot(weights, inverse.T, precision=HIGHEST, preferred_element_type=jnp.float32)
    half = lax.all_gather(
        back_rows.astype(jnp.bfloat16), "row", axis_index_groups=along_z, tiled=True
    )
    squares = jnp.sum(jnp.square(half.astype(jnp.float32)), axis=0).reshape(BLOCKS, BLOCK)
    squares = squares + lax.ppermute(squares, "row", other)
    squares, projected, inverse = lax.optimization_barrier((squares, projected, inverse))
    squares = exchange(squares, "col", None, n_col)
    right_bf = both_halves(half)
    left_bf = jnp.dot(
        projected, inverse.T, precision=HIGHEST, preferred_element_type=jnp.float32
    ).astype(jnp.bfloat16)
    correction = lax.dot_general(
        left_bf, right_bf, (((1,), (1,)), ((), ())), preferred_element_type=jnp.float32
    )
    new_momentum = (blended.astype(jnp.float32) - FEEDBACK * correction).astype(jnp.bfloat16)
    squares, new_momentum = lax.optimization_barrier((squares, new_momentum))
    back_squares = jnp.sum(squares, axis=0).reshape(RANK)
    scale = (1.0 / jnp.sqrt(back_squares / COLS + NORM_EPS)).reshape(1, RANK)
    new_factor, weight_update = finish(scale, right_bf, left_bf)
    return (new_momentum, weight_update, new_factor)


def solution(mesh):
    placed = (P("row", "col"), P("row", "col"), P("col", None))
    return jax.shard_map(
        local,
        mesh=mesh,
        in_specs=placed,
        out_specs=(P("row", "col"), P("row", "col"), P("col", None)),
        check_vma=False,
    )
```

```python
import math

import jax
import jax.numpy as jnp
from jax import lax
from jax.experimental import pallas as pl
from jax.experimental.pallas import tpu as pltpu
from jax.sharding import PartitionSpec as P

ROWS = 8192
COLS = 26624
RANK = 512


NORM_EPS = 1e-06
GRAM_JITTER = 0.0001
FEEDBACK = 0.25

HIGHEST = lax.Precision.HIGHEST
BLOCK = 128
BLOCKS = RANK // BLOCK
SUB = 8
GROUPS = BLOCK // SUB
PAIRS = [(i, j) for i in range(BLOCKS) for j in range(i, BLOCKS)]


def sub_row(x, k):
    return jnp.broadcast_to(x[k : k + 1, :], (SUB, BLOCK))


def lane_col(x, c):
    return jnp.broadcast_to(x[:, c : c + 1], (SUB, BLOCK))


def pieces(x):
    hi = x.astype(jnp.bfloat16)
    rest = x - hi.astype(jnp.float32)
    mid = rest.astype(jnp.bfloat16)
    return hi, mid, (rest - mid.astype(jnp.float32)).astype(jnp.bfloat16)


def stacked(*parts):
    return jnp.concatenate([x.astype(jnp.float32) for x in parts], axis=0).astype(jnp.bfloat16)


def factor_block(rows):
    sub = lax.broadcasted_iota(jnp.int32, (SUB, BLOCK), 0)
    lane = lax.broadcasted_iota(jnp.int32, (SUB, BLOCK), 1)
    out = []
    for p in range(GROUPS):
        panel = (lane >= SUB * p) & (lane < SUB * (p + 1))
        cols = [lane_col(rows[p], SUB * p + j) for j in range(SUB)]
        x = jnp.where(panel, jnp.where(lane == sub + SUB * p, 1.0, 0.0), rows[p])
        pivots, recips, row_k, upper = [], [], [], []
        for k in range(SUB):
            pivot = sub_row(cols[k], k)
            r = pl.reciprocal(pivot, approx=True)
            m = jnp.where(sub > k, cols[k] * r, 0.0)
            u = {j: sub_row(cols[j], k) for j in range(k + 1, SUB)}
            for j in range(k + 1, SUB):
                cols[j] = cols[j] - m * u[j]
            xk = sub_row(x, k)
            if k < SUB - 1:
                x = x - m * xk
            pivots.append(pivot)
            recips.append(r)
            row_k.append(xk)
            upper.append(u)
        d8 = pivots[0]
        for k in range(1, SUB):
            d8 = jnp.where(sub == k, pivots[k], d8)
        out.append(jnp.where(lane < SUB * (p + 1), x * lax.rsqrt(d8), 0.0))
        if p + 1 < GROUPS:
            b = [lane_col(rows[p + 1], SUB * p + j) for j in range(SUB)]
            y = jnp.where(panel, 0.0, rows[p + 1])
            for k in range(SUB):
                m = b[k] * recips[k]
                for j in range(k + 1, SUB):
                    b[j] = b[j] - m * upper[k][j]
                y = y - m * row_k[k]
            rows[p + 1] = y
        if p + 2 < GROUPS:
            r8 = recips[0]
            for k in range(1, SUB):
                r8 = jnp.where(sub == k, recips[k], r8)
            hi, mid, low = pieces(x)
            hi2, mid2, low2 = pieces(x * r8)
            product = lax.dot_general(
                stacked(hi, hi, mid, mid, hi, low),
                stacked(hi2, mid2, hi2, mid2, low2, hi2),
                (((0,), (0,)), ((), ())),
                preferred_element_type=jnp.float32,
            )
            for q in range(p + 2, GROUPS):
                rows[q] = jnp.where(panel, 0.0, rows[q]) - product[SUB * q : SUB * (q + 1), :]
    return out


def inverse_factor_kernel(core_ref, mine_ref, theirs_ref, m_ref, s_ref, d_ref, x_ref, y_ref):
    half = mine_ref.shape[0]

    def gram(n):
        return jnp.where(core_ref[0] == n // half, mine_ref[n % half], theirs_ref[n % half])

    eye = (
        lax.broadcasted_iota(jnp.int32, (BLOCK, BLOCK), 0)
        == lax.broadcasted_iota(jnp.int32, (BLOCK, BLOCK), 1)
    )
    diagonal = jnp.zeros((BLOCK, BLOCK), jnp.float32)
    for n, (i, j) in enumerate(PAIRS):
        if i == j:
            diagonal += jnp.where(eye, gram(n), 0.0)
    jitter = (GRAM_JITTER / RANK) * jnp.sum(diagonal)
    s_ref[...] = jnp.zeros_like(s_ref)
    for n, (i, j) in enumerate(PAIRS):
        x = gram(n)
        if i == j:
            x = x + jnp.where(eye, jitter, 0.0)
        s_ref[BLOCK * i : BLOCK * (i + 1), BLOCK * j : BLOCK * (j + 1)] = x

    def block(b, carry):
        lo = pl.multiple_of(b * BLOCK, BLOCK)
        rows = [s_ref[pl.ds(lo + SUB * q, SUB), pl.ds(lo, BLOCK)] for q in range(GROUPS)]
        for q, x in enumerate(factor_block(rows)):
            d_ref[SUB * q : SUB * (q + 1), :] = x
        m_bb = d_ref[...]
        hi, mid, low = pieces(m_bb)
        first = jnp.concatenate([hi, hi, mid, mid, hi, low], axis=1)
        hi, mid, low = pieces(s_ref[pl.ds(lo, BLOCK), :])
        second = jnp.concatenate([hi, mid, hi, mid, low, hi], axis=0)
        s_ref[pl.ds(lo, BLOCK), :] = jnp.dot(first, second, preferred_element_type=jnp.float32)
        s_ref[pl.ds(lo, BLOCK), pl.ds(lo, BLOCK)] = m_bb
        hi, mid, low = pieces(s_ref[pl.ds(lo, BLOCK), :])
        for n, (x, y) in enumerate(((hi, hi), (hi, mid), (mid, hi), (mid, mid), (hi, low), (low, hi))):
            x_ref[BLOCK * n : BLOCK * (n + 1), :] = x
            y_ref[BLOCK * n : BLOCK * (n + 1), :] = y
        for i in range(1, BLOCKS):

            @pl.when(i > b)
            def _():
                here = slice(BLOCK * i, BLOCK * (i + 1))
                s_ref[here, pl.ds(lo, BLOCK)] = jnp.zeros((BLOCK, BLOCK), jnp.float32)
                s_ref[here, :] -= lax.dot_general(
                    x_ref[:, here], y_ref[...], (((0,), (0,)), ((), ())), preferred_element_type=jnp.float32
                )

        return carry

    lax.fori_loop(0, BLOCKS, block, 0)
    for i in range(BLOCKS):
        for j in range(BLOCKS):
            here = (slice(BLOCK * i, BLOCK * (i + 1)), slice(BLOCK * j, BLOCK * (j + 1)))
            m_ref[here] = s_ref[here] if j <= i else jnp.zeros((BLOCK, BLOCK), jnp.float32)


def gram_kernel(p_ref, o_ref):
    for i in range(BLOCKS):
        rows = lax.dot_general(
            p_ref[:, BLOCK * i : BLOCK * (i + 1)],
            p_ref[:, BLOCK * i :],
            (((0,), (0,)), ((), ())),
            precision=HIGHEST,
            preferred_element_type=jnp.float32,
        )
        for j in range(i, BLOCKS):
            o_ref[PAIRS.index((i, j))] = rows[:, BLOCK * (j - i) : BLOCK * (j - i + 1)]


def gram_blocks(projected):
    return pl.pallas_call(
        gram_kernel,
        out_shape=jax.ShapeDtypeStruct((len(PAIRS), BLOCK, BLOCK), jnp.float32),
        in_specs=[pl.BlockSpec(memory_space=pltpu.VMEM)],
        out_specs=pl.BlockSpec(memory_space=pltpu.VMEM),
        compiler_params=pltpu.CompilerParams(vmem_limit_bytes=16 * 1024 * 1024),
        cost_estimate=pl.CostEstimate(flops=2**31, bytes_accessed=2**21, transcendentals=0),
    )(projected)


def inverse_factor(core, mine, theirs):
    return pl.pallas_call(
        inverse_factor_kernel,
        out_shape=jax.ShapeDtypeStruct((RANK, RANK), jnp.float32),
        in_specs=[pl.BlockSpec(memory_space=pltpu.SMEM)] + [pl.BlockSpec(memory_space=pltpu.VMEM)] * 2,
        out_specs=pl.BlockSpec(memory_space=pltpu.VMEM),
        scratch_shapes=[
            pltpu.VMEM((RANK, RANK), jnp.float32),
            pltpu.VMEM((BLOCK, BLOCK), jnp.float32),
            pltpu.VMEM((6 * BLOCK, RANK), jnp.bfloat16),
            pltpu.VMEM((6 * BLOCK, RANK), jnp.bfloat16),
        ],
        compiler_params=pltpu.CompilerParams(vmem_limit_bytes=16 * 1024 * 1024),
        cost_estimate=pl.CostEstimate(flops=25 * 10**9, bytes_accessed=2**21, transcendentals=0),
    )(core.astype(jnp.int32).reshape(1), mine, theirs)


def weights_kernel(half_ref, b_ref, p_ref, *refs):
    *added, o_ref, w_ref = refs
    start = b_ref.shape[1] - w_ref.shape[0]
    half = half_ref[0]
    rows = b_ref[:, pl.ds(pl.multiple_of(half * start, BLOCK), w_ref.shape[0])]
    for n, piece in enumerate(pieces(p_ref[...])):
        term = lax.dot_general(rows, piece, (((0,), (0,)), ((), ())), preferred_element_type=jnp.float32)
        w_ref[...] = term if n == 0 else w_ref[...] + term
    own = w_ref[pl.ds(pl.multiple_of(half * (o_ref.shape[0] - start), SUB), o_ref.shape[0]), :]
    o_ref[...] = own + added[0][...] if added else own


def weights_half(half, blended, projected, *added):
    rows = blended.shape[1] // 2
    start = rows // BLOCK * BLOCK
    vmem = pl.BlockSpec(memory_space=pltpu.VMEM)
    return pl.pallas_call(
        weights_kernel,
        out_shape=jax.ShapeDtypeStruct((rows, RANK), jnp.float32),
        in_specs=[pl.BlockSpec(memory_space=pltpu.SMEM)] + [vmem] * (2 + len(added)),
        out_specs=vmem,
        scratch_shapes=[pltpu.VMEM((blended.shape[1] - start, RANK), jnp.float32)],
        compiler_params=pltpu.CompilerParams(vmem_limit_bytes=32 * 1024 * 1024),
        cost_estimate=pl.CostEstimate(flops=2**31, bytes_accessed=2**22, transcendentals=0),
    )(half.astype(jnp.int32).reshape(1), blended, projected, *added)


def scatter_sum(x, axis, size):
    parts = x.reshape((size, x.shape[0] // size) + x.shape[1:])
    return jnp.sum(lax.all_to_all(parts, axis, 0, 0), axis=0)


def exchange(x, axis, groups, size):
    return lax.all_to_all(jnp.broadcast_to(x, (size,) + x.shape), axis, 0, 0, axis_index_groups=groups)


def local(momentum, gradient, right_factor):
    n_col = lax.axis_size("col")
    n_row = lax.axis_size("row")
    n_z = n_row // 2
    core = lax.axis_index("row") % 2
    other = [(i, i ^ 1) for i in range(n_row)]
    along_z = [[2 * z + c for z in range(n_z)] for c in range(2)]

    def both_halves(mine):
        theirs = lax.ppermute(mine, "row", other)
        return jnp.concatenate([jnp.where(core == 0, mine, theirs), jnp.where(core == 0, theirs, mine)])

    blended = (momentum.astype(jnp.float32) + gradient.astype(jnp.float32)).astype(jnp.bfloat16)
    partial_proj = jnp.dot(blended, right_factor, preferred_element_type=jnp.float32)
    projected = exchange(scatter_sum(partial_proj, "col", n_col), "col", None, n_col).reshape(partial_proj.shape)

    theirs = weights_half(1 - core, blended, projected)
    theirs, projected = lax.optimization_barrier((theirs, projected))
    theirs = lax.ppermute(theirs, "row", other)

    packed = gram_blocks(projected).reshape(2, len(PAIRS) // 2 * BLOCK, BLOCK)
    share = packed.shape[1] // n_col
    here = lax.axis_index("col") * share
    mine, for_other = (
        lax.dynamic_slice(packed, (which, here, 0), (1, share, BLOCK))[0] for which in (core, 1 - core)
    )
    packed = mine + lax.ppermute(for_other, "row", other)

    weights = weights_half(core, blended, projected, theirs)
    weights = lax.psum_scatter(
        weights, "row", scatter_dimension=0, axis_index_groups=along_z, tiled=True
    )
    packed = jnp.sum(exchange(packed, "row", along_z, n_z), axis=0)
    packed = exchange(packed, "col", None, n_col).reshape(len(PAIRS) // 2, BLOCK, BLOCK)

    inverse = inverse_factor(core, packed, lax.ppermute(packed, "row", other))
    left_bf = jnp.dot(
        projected, inverse.T, precision=HIGHEST, preferred_element_type=jnp.float32
    ).astype(jnp.bfloat16)
    left_bf, weights = lax.optimization_barrier((left_bf, weights))
    back_rows = jnp.dot(weights, inverse.T, precision=HIGHEST, preferred_element_type=jnp.float32)
    half = lax.all_gather(
        back_rows.astype(jnp.bfloat16), "row", axis_index_groups=along_z, tiled=True
    )
    squares = jnp.sum(jnp.square(half.astype(jnp.float32)), axis=0).reshape(BLOCKS, BLOCK)
    squares = squares + lax.ppermute(squares, "row", other)
    squares = exchange(squares, "col", None, n_col)
    right_bf = both_halves(half)
    correction = lax.dot_general(
        left_bf, right_bf, (((1,), (1,)), ((), ())), preferred_element_type=jnp.float32
    )
    new_momentum = (blended.astype(jnp.float32) - FEEDBACK * correction).astype(jnp.bfloat16)
    squares, new_momentum = lax.optimization_barrier((squares, new_momentum))
    back_squares = jnp.sum(squares, axis=0).reshape(RANK)
    new_factor = right_bf.astype(jnp.float32) * (1.0 / jnp.sqrt(back_squares / COLS + NORM_EPS))
    factor_bf = new_factor.astype(jnp.bfloat16)
    update_full = lax.dot_general(
        left_bf, factor_bf, (((1,), (1,)), ((), ())), preferred_element_type=jnp.float32
    )
    weight_update = (update_full * math.sqrt(ROWS / RANK)).astype(jnp.bfloat16)
    return (new_momentum, weight_update, new_factor)


def solution(mesh):
    placed = (P("row", "col"), P("row", "col"), P("col", None))
    return jax.shard_map(
        local,
        mesh=mesh,
        in_specs=placed,
        out_specs=(P("row", "col"), P("row", "col"), P("col", None)),
        check_vma=False,
    )
```

```python
import math

import jax
import jax.numpy as jnp
from jax import lax
from jax.experimental import pallas as pl
from jax.experimental.pallas import tpu as pltpu
from jax.sharding import PartitionSpec as P

ROWS = 8192
COLS = 26624
RANK = 512


NORM_EPS = 1e-06
GRAM_JITTER = 0.0001
FEEDBACK = 0.25

HIGHEST = lax.Precision.HIGHEST
BLOCK = 128
BLOCKS = RANK // BLOCK
SUB = 8
GROUPS = BLOCK // SUB
PAIRS = [(i, j) for i in range(BLOCKS) for j in range(i, BLOCKS)]


def sub_row(x, k):
    return jnp.broadcast_to(x[k : k + 1, :], (SUB, BLOCK))


def lane_col(x, c):
    return jnp.broadcast_to(x[:, c : c + 1], (SUB, BLOCK))


def pieces(x):
    hi = x.astype(jnp.bfloat16)
    rest = x - hi.astype(jnp.float32)
    mid = rest.astype(jnp.bfloat16)
    return hi, mid, (rest - mid.astype(jnp.float32)).astype(jnp.bfloat16)


def stacked(*parts):
    return jnp.concatenate([x.astype(jnp.float32) for x in parts], axis=0).astype(jnp.bfloat16)


def factor_block(rows):
    sub = lax.broadcasted_iota(jnp.int32, (SUB, BLOCK), 0)
    lane = lax.broadcasted_iota(jnp.int32, (SUB, BLOCK), 1)
    out = []
    for p in range(GROUPS):
        panel = (lane >= SUB * p) & (lane < SUB * (p + 1))
        cols = [lane_col(rows[p], SUB * p + j) for j in range(SUB)]
        x = jnp.where(panel, jnp.where(lane == sub + SUB * p, 1.0, 0.0), rows[p])
        pivots, recips, row_k, upper = [], [], [], []
        for k in range(SUB):
            pivot = sub_row(cols[k], k)
            r = pl.reciprocal(pivot, approx=True)
            m = jnp.where(sub > k, cols[k] * r, 0.0)
            u = {j: sub_row(cols[j], k) for j in range(k + 1, SUB)}
            for j in range(k + 1, SUB):
                cols[j] = cols[j] - m * u[j]
            xk = sub_row(x, k)
            if k < SUB - 1:
                x = x - m * xk
            pivots.append(pivot)
            recips.append(r)
            row_k.append(xk)
            upper.append(u)
        d8 = pivots[0]
        for k in range(1, SUB):
            d8 = jnp.where(sub == k, pivots[k], d8)
        out.append(jnp.where(lane < SUB * (p + 1), x * lax.rsqrt(d8), 0.0))
        if p + 1 < GROUPS:
            b = [lane_col(rows[p + 1], SUB * p + j) for j in range(SUB)]
            y = jnp.where(panel, 0.0, rows[p + 1])
            for k in range(SUB):
                m = b[k] * recips[k]
                for j in range(k + 1, SUB):
                    b[j] = b[j] - m * upper[k][j]
                y = y - m * row_k[k]
            rows[p + 1] = y
        if p + 2 < GROUPS:
            r8 = recips[0]
            for k in range(1, SUB):
                r8 = jnp.where(sub == k, recips[k], r8)
            hi, mid, low = pieces(x)
            hi2, mid2, low2 = pieces(x * r8)
            product = lax.dot_general(
                stacked(hi, hi, mid, mid, hi, low),
                stacked(hi2, mid2, hi2, mid2, low2, hi2),
                (((0,), (0,)), ((), ())),
                preferred_element_type=jnp.float32,
            )
            for q in range(p + 2, GROUPS):
                rows[q] = jnp.where(panel, 0.0, rows[q]) - product[SUB * q : SUB * (q + 1), :]
    return out


def inverse_factor_kernel(core_ref, mine_ref, theirs_ref, m_ref, s_ref, d_ref, x_ref, y_ref):
    half = mine_ref.shape[0]

    def gram(n):
        return jnp.where(core_ref[0] == n // half, mine_ref[n % half], theirs_ref[n % half])

    eye = (
        lax.broadcasted_iota(jnp.int32, (BLOCK, BLOCK), 0)
        == lax.broadcasted_iota(jnp.int32, (BLOCK, BLOCK), 1)
    )
    diagonal = jnp.zeros((BLOCK, BLOCK), jnp.float32)
    for n, (i, j) in enumerate(PAIRS):
        if i == j:
            diagonal += jnp.where(eye, gram(n), 0.0)
    jitter = (GRAM_JITTER / RANK) * jnp.sum(diagonal)
    s_ref[...] = jnp.zeros_like(s_ref)
    for n, (i, j) in enumerate(PAIRS):
        x = gram(n)
        if i == j:
            x = x + jnp.where(eye, jitter, 0.0)
        s_ref[BLOCK * i : BLOCK * (i + 1), BLOCK * j : BLOCK * (j + 1)] = x

    def block(b, carry):
        lo = pl.multiple_of(b * BLOCK, BLOCK)
        rows = [s_ref[pl.ds(lo + SUB * q, SUB), pl.ds(lo, BLOCK)] for q in range(GROUPS)]
        for q, x in enumerate(factor_block(rows)):
            d_ref[SUB * q : SUB * (q + 1), :] = x
        m_bb = d_ref[...]
        hi, mid, low = pieces(m_bb)
        first = jnp.concatenate([hi, hi, mid, mid, hi, low], axis=1)
        hi, mid, low = pieces(s_ref[pl.ds(lo, BLOCK), :])
        second = jnp.concatenate([hi, mid, hi, mid, low, hi], axis=0)
        s_ref[pl.ds(lo, BLOCK), :] = jnp.dot(first, second, preferred_element_type=jnp.float32)
        s_ref[pl.ds(lo, BLOCK), pl.ds(lo, BLOCK)] = m_bb
        hi, mid, low = pieces(s_ref[pl.ds(lo, BLOCK), :])
        for n, (x, y) in enumerate(((hi, hi), (hi, mid), (mid, hi), (mid, mid), (hi, low), (low, hi))):
            x_ref[BLOCK * n : BLOCK * (n + 1), :] = x
            y_ref[BLOCK * n : BLOCK * (n + 1), :] = y
        for i in range(1, BLOCKS):

            @pl.when(i > b)
            def _():
                here = slice(BLOCK * i, BLOCK * (i + 1))
                s_ref[here, pl.ds(lo, BLOCK)] = jnp.zeros((BLOCK, BLOCK), jnp.float32)
                s_ref[here, :] -= lax.dot_general(
                    x_ref[:, here], y_ref[...], (((0,), (0,)), ((), ())), preferred_element_type=jnp.float32
                )

        return carry

    lax.fori_loop(0, BLOCKS, block, 0)
    for i in range(BLOCKS):
        for j in range(BLOCKS):
            here = (slice(BLOCK * i, BLOCK * (i + 1)), slice(BLOCK * j, BLOCK * (j + 1)))
            m_ref[here] = s_ref[here] if j <= i else jnp.zeros((BLOCK, BLOCK), jnp.float32)


def gram_kernel(p_ref, o_ref):
    for i in range(BLOCKS):
        rows = lax.dot_general(
            p_ref[:, BLOCK * i : BLOCK * (i + 1)],
            p_ref[:, BLOCK * i :],
            (((0,), (0,)), ((), ())),
            precision=HIGHEST,
            preferred_element_type=jnp.float32,
        )
        for j in range(i, BLOCKS):
            o_ref[PAIRS.index((i, j))] = rows[:, BLOCK * (j - i) : BLOCK * (j - i + 1)]


def gram_blocks(projected):
    return pl.pallas_call(
        gram_kernel,
        out_shape=jax.ShapeDtypeStruct((len(PAIRS), BLOCK, BLOCK), jnp.float32),
        in_specs=[pl.BlockSpec(memory_space=pltpu.VMEM)],
        out_specs=pl.BlockSpec(memory_space=pltpu.VMEM),
        compiler_params=pltpu.CompilerParams(vmem_limit_bytes=16 * 1024 * 1024),
        cost_estimate=pl.CostEstimate(flops=2**31, bytes_accessed=2**21, transcendentals=0),
    )(projected)


def inverse_factor(core, mine, theirs):
    return pl.pallas_call(
        inverse_factor_kernel,
        out_shape=jax.ShapeDtypeStruct((RANK, RANK), jnp.float32),
        in_specs=[pl.BlockSpec(memory_space=pltpu.SMEM)] + [pl.BlockSpec(memory_space=pltpu.VMEM)] * 2,
        out_specs=pl.BlockSpec(memory_space=pltpu.VMEM),
        scratch_shapes=[
            pltpu.VMEM((RANK, RANK), jnp.float32),
            pltpu.VMEM((BLOCK, BLOCK), jnp.float32),
            pltpu.VMEM((6 * BLOCK, RANK), jnp.bfloat16),
            pltpu.VMEM((6 * BLOCK, RANK), jnp.bfloat16),
        ],
        compiler_params=pltpu.CompilerParams(vmem_limit_bytes=16 * 1024 * 1024),
        cost_estimate=pl.CostEstimate(flops=25 * 10**9, bytes_accessed=2**21, transcendentals=0),
    )(core.astype(jnp.int32).reshape(1), mine, theirs)


def weights_kernel(half_ref, b_ref, p_ref, *refs):
    *added, o_ref, w_ref = refs
    start = b_ref.shape[1] - w_ref.shape[0]
    half = half_ref[0]
    rows = b_ref[:, pl.ds(pl.multiple_of(half * start, BLOCK), w_ref.shape[0])]
    w_ref[...] = lax.dot_general(
        jnp.concatenate([rows] * 3, axis=0),
        jnp.concatenate(pieces(p_ref[...]), axis=0),
        (((0,), (0,)), ((), ())),
        preferred_element_type=jnp.float32,
    )
    own = w_ref[pl.ds(pl.multiple_of(half * (o_ref.shape[0] - start), SUB), o_ref.shape[0]), :]
    o_ref[...] = own + added[0][...] if added else own


def weights_half(half, blended, projected, *added):
    rows = blended.shape[1] // 2
    start = rows // BLOCK * BLOCK
    vmem = pl.BlockSpec(memory_space=pltpu.VMEM)
    return pl.pallas_call(
        weights_kernel,
        out_shape=jax.ShapeDtypeStruct((rows, RANK), jnp.float32),
        in_specs=[pl.BlockSpec(memory_space=pltpu.SMEM)] + [vmem] * (2 + len(added)),
        out_specs=vmem,
        scratch_shapes=[pltpu.VMEM((blended.shape[1] - start, RANK), jnp.float32)],
        compiler_params=pltpu.CompilerParams(vmem_limit_bytes=32 * 1024 * 1024),
        cost_estimate=pl.CostEstimate(flops=2**31, bytes_accessed=2**22, transcendentals=0),
    )(half.astype(jnp.int32).reshape(1), blended, projected, *added)


def finish_kernel(scale_ref, left_ref, right_hbm, factor_hbm, update_hbm, right_ref, factor_ref, update_ref, sems):
    total = right_ref.shape[0]
    cut = (total // BLOCK + 1) // 2 * BLOCK
    chunks = (slice(0, cut), slice(cut, total))
    arrivals = [
        pltpu.make_async_copy(right_hbm.at[chunk, :], right_ref.at[chunk, :], sems.at[n])
        for n, chunk in enumerate(chunks)
    ]
    for copy in arrivals:
        copy.start()
    leaving = []
    for n, chunk in enumerate(chunks):
        arrivals[n].wait()
        factor_ref[chunk, :] = right_ref[chunk, :].astype(jnp.float32) * scale_ref[...]
        leaving.append(
            pltpu.make_async_copy(factor_ref.at[chunk, :], factor_hbm.at[chunk, :], sems.at[2 + n])
        )
        leaving[-1].start()
        update = lax.dot_general(
            left_ref[...],
            factor_ref[chunk, :].astype(jnp.bfloat16),
            (((1,), (1,)), ((), ())),
            preferred_element_type=jnp.float32,
        )
        update_ref[:, chunk] = (update * math.sqrt(ROWS / RANK)).astype(jnp.bfloat16)
        leaving.append(
            pltpu.make_async_copy(update_ref.at[:, chunk], update_hbm.at[:, chunk], sems.at[4 + n])
        )
        leaving[-1].start()
    for copy in leaving:
        copy.wait()


def finish(scale, left_bf, right_bf):
    factor = jax.ShapeDtypeStruct(right_bf.shape, jnp.float32)
    update = jax.ShapeDtypeStruct((left_bf.shape[0], right_bf.shape[0]), jnp.bfloat16)
    vmem, hbm = pl.BlockSpec(memory_space=pltpu.VMEM), pl.BlockSpec(memory_space=pl.ANY)
    return pl.pallas_call(
        finish_kernel,
        out_shape=(factor, update),
        in_specs=[vmem, vmem, hbm],
        out_specs=(hbm, hbm),
        scratch_shapes=[
            pltpu.VMEM(right_bf.shape, right_bf.dtype),
            pltpu.VMEM(factor.shape, factor.dtype),
            pltpu.VMEM(update.shape, update.dtype),
            pltpu.SemaphoreType.DMA((6,)),
        ],
        compiler_params=pltpu.CompilerParams(vmem_limit_bytes=56 * 1024 * 1024),
        cost_estimate=pl.CostEstimate(flops=2**30, bytes_accessed=2**23, transcendentals=0),
    )(scale, left_bf, right_bf)


def scatter_sum(x, axis, size):
    parts = x.reshape((size, x.shape[0] // size) + x.shape[1:])
    return jnp.sum(lax.all_to_all(parts, axis, 0, 0), axis=0)


def exchange(x, axis, groups, size):
    return lax.all_to_all(jnp.broadcast_to(x, (size,) + x.shape), axis, 0, 0, axis_index_groups=groups)


def local(momentum, gradient, right_factor):
    n_col = lax.axis_size("col")
    n_row = lax.axis_size("row")
    n_z = n_row // 2
    core = lax.axis_index("row") % 2
    other = [(i, i ^ 1) for i in range(n_row)]
    along_z = [[2 * z + c for z in range(n_z)] for c in range(2)]

    def both_halves(mine):
        theirs = lax.ppermute(mine, "row", other)
        return jnp.concatenate([jnp.where(core == 0, mine, theirs), jnp.where(core == 0, theirs, mine)])

    blended = (momentum.astype(jnp.float32) + gradient.astype(jnp.float32)).astype(jnp.bfloat16)
    partial_proj = jnp.dot(blended, right_factor, preferred_element_type=jnp.float32)
    projected = exchange(scatter_sum(partial_proj, "col", n_col), "col", None, n_col).reshape(partial_proj.shape)

    theirs = weights_half(1 - core, blended, projected)
    theirs, projected = lax.optimization_barrier((theirs, projected))
    theirs = lax.ppermute(theirs, "row", other)

    packed = gram_blocks(projected).reshape(2, len(PAIRS) // 2 * BLOCK, BLOCK)
    share = packed.shape[1] // n_col
    here = lax.axis_index("col") * share
    mine, for_other = (
        lax.dynamic_slice(packed, (which, here, 0), (1, share, BLOCK))[0] for which in (core, 1 - core)
    )
    packed = mine + lax.ppermute(for_other, "row", other)

    weights = weights_half(core, blended, projected, theirs)
    weights = lax.psum_scatter(
        weights, "row", scatter_dimension=0, axis_index_groups=along_z, tiled=True
    )
    packed = jnp.sum(exchange(packed, "row", along_z, n_z), axis=0)
    packed = exchange(packed, "col", None, n_col).reshape(len(PAIRS) // 2, BLOCK, BLOCK)

    inverse = inverse_factor(core, packed, lax.ppermute(packed, "row", other))
    left_bf = jnp.dot(
        projected, inverse.T, precision=HIGHEST, preferred_element_type=jnp.float32
    ).astype(jnp.bfloat16)
    left_bf, weights = lax.optimization_barrier((left_bf, weights))
    back_rows = jnp.dot(weights, inverse.T, precision=HIGHEST, preferred_element_type=jnp.float32)
    half = lax.all_gather(
        back_rows.astype(jnp.bfloat16), "row", axis_index_groups=along_z, tiled=True
    )
    squares = jnp.sum(jnp.square(half.astype(jnp.float32)), axis=0).reshape(BLOCKS, BLOCK)
    squares = squares + lax.ppermute(squares, "row", other)
    squares = exchange(squares, "col", None, n_col)
    right_bf = both_halves(half)
    correction = lax.dot_general(
        left_bf, right_bf, (((1,), (1,)), ((), ())), preferred_element_type=jnp.float32
    )
    new_momentum = (blended.astype(jnp.float32) - FEEDBACK * correction).astype(jnp.bfloat16)
    squares, new_momentum = lax.optimization_barrier((squares, new_momentum))
    back_squares = jnp.sum(squares, axis=0).reshape(RANK)
    scale = (1.0 / jnp.sqrt(back_squares / COLS + NORM_EPS)).reshape(1, RANK)
    new_factor, weight_update = finish(scale, left_bf, right_bf)
    return (new_momentum, weight_update, new_factor)


def solution(mesh):
    placed = (P("row", "col"), P("row", "col"), P("col", None))
    return jax.shard_map(
        local,
        mesh=mesh,
        in_specs=placed,
        out_specs=(P("row", "col"), P("row", "col"), P("col", None)),
        check_vma=False,
    )
```

```python
import math

import jax
import jax.numpy as jnp
from jax import lax
from jax.experimental import pallas as pl
from jax.experimental.pallas import tpu as pltpu
from jax.sharding import PartitionSpec as P

ROWS = 8192
COLS = 26624
RANK = 512


NORM_EPS = 1e-06
GRAM_JITTER = 0.0001
FEEDBACK = 0.25

HIGHEST = lax.Precision.HIGHEST
BLOCK = 128
BLOCKS = RANK // BLOCK
SUB = 8
GROUPS = BLOCK // SUB
PAIRS = [(i, j) for i in range(BLOCKS) for j in range(i, BLOCKS)]


def sub_row(x, k):
    return jnp.broadcast_to(x[k : k + 1, :], (SUB, BLOCK))


def lane_col(x, c):
    return jnp.broadcast_to(x[:, c : c + 1], (SUB, BLOCK))


def pieces(x):
    hi = x.astype(jnp.bfloat16)
    rest = x - hi.astype(jnp.float32)
    mid = rest.astype(jnp.bfloat16)
    return hi, mid, (rest - mid.astype(jnp.float32)).astype(jnp.bfloat16)


def stacked(*parts):
    return jnp.concatenate([x.astype(jnp.float32) for x in parts], axis=0).astype(jnp.bfloat16)


def factor_block(rows):
    sub = lax.broadcasted_iota(jnp.int32, (SUB, BLOCK), 0)
    lane = lax.broadcasted_iota(jnp.int32, (SUB, BLOCK), 1)
    out = []
    for p in range(GROUPS):
        panel = (lane >= SUB * p) & (lane < SUB * (p + 1))
        cols = [lane_col(rows[p], SUB * p + j) for j in range(SUB)]
        x = jnp.where(panel, jnp.where(lane == sub + SUB * p, 1.0, 0.0), rows[p])
        pivots, recips, row_k, upper = [], [], [], []
        for k in range(SUB):
            pivot = sub_row(cols[k], k)
            r = pl.reciprocal(pivot, approx=True)
            m = jnp.where(sub > k, cols[k] * r, 0.0)
            u = {j: sub_row(cols[j], k) for j in range(k + 1, SUB)}
            for j in range(k + 1, SUB):
                cols[j] = cols[j] - m * u[j]
            xk = sub_row(x, k)
            if k < SUB - 1:
                x = x - m * xk
            pivots.append(pivot)
            recips.append(r)
            row_k.append(xk)
            upper.append(u)
        d8 = pivots[0]
        for k in range(1, SUB):
            d8 = jnp.where(sub == k, pivots[k], d8)
        out.append(jnp.where(lane < SUB * (p + 1), x * lax.rsqrt(d8), 0.0))
        if p + 1 < GROUPS:
            b = [lane_col(rows[p + 1], SUB * p + j) for j in range(SUB)]
            y = jnp.where(panel, 0.0, rows[p + 1])
            for k in range(SUB):
                m = b[k] * recips[k]
                for j in range(k + 1, SUB):
                    b[j] = b[j] - m * upper[k][j]
                y = y - m * row_k[k]
            rows[p + 1] = y
        if p + 2 < GROUPS:
            r8 = recips[0]
            for k in range(1, SUB):
                r8 = jnp.where(sub == k, recips[k], r8)
            hi, mid, low = pieces(x)
            hi2, mid2, low2 = pieces(x * r8)
            product = lax.dot_general(
                stacked(hi, hi, mid, mid, hi, low),
                stacked(hi2, mid2, hi2, mid2, low2, hi2),
                (((0,), (0,)), ((), ())),
                preferred_element_type=jnp.float32,
            )
            for q in range(p + 2, GROUPS):
                rows[q] = jnp.where(panel, 0.0, rows[q]) - product[SUB * q : SUB * (q + 1), :]
    return out


def inverse_factor_kernel(core_ref, mine_ref, theirs_ref, m_ref, s_ref, d_ref, x_ref, y_ref):
    half = mine_ref.shape[0]

    def gram(n):
        return jnp.where(core_ref[0] == n // half, mine_ref[n % half], theirs_ref[n % half])

    eye = (
        lax.broadcasted_iota(jnp.int32, (BLOCK, BLOCK), 0)
        == lax.broadcasted_iota(jnp.int32, (BLOCK, BLOCK), 1)
    )
    diagonal = jnp.zeros((BLOCK, BLOCK), jnp.float32)
    for n, (i, j) in enumerate(PAIRS):
        if i == j:
            diagonal += jnp.where(eye, gram(n), 0.0)
    jitter = (GRAM_JITTER / RANK) * jnp.sum(diagonal)
    s_ref[...] = jnp.zeros_like(s_ref)
    for n, (i, j) in enumerate(PAIRS):
        x = gram(n)
        if i == j:
            x = x + jnp.where(eye, jitter, 0.0)
        s_ref[BLOCK * i : BLOCK * (i + 1), BLOCK * j : BLOCK * (j + 1)] = x

    def block(b, carry):
        lo = pl.multiple_of(b * BLOCK, BLOCK)
        rows = [s_ref[pl.ds(lo + SUB * q, SUB), pl.ds(lo, BLOCK)] for q in range(GROUPS)]
        for q, x in enumerate(factor_block(rows)):
            d_ref[SUB * q : SUB * (q + 1), :] = x
        m_bb = d_ref[...]
        hi, mid, low = pieces(m_bb)
        first = jnp.concatenate([hi, hi, mid, mid, hi, low], axis=1)
        hi, mid, low = pieces(s_ref[pl.ds(lo, BLOCK), :])
        second = jnp.concatenate([hi, mid, hi, mid, low, hi], axis=0)
        s_ref[pl.ds(lo, BLOCK), :] = jnp.dot(first, second, preferred_element_type=jnp.float32)
        s_ref[pl.ds(lo, BLOCK), pl.ds(lo, BLOCK)] = m_bb
        hi, mid, low = pieces(s_ref[pl.ds(lo, BLOCK), :])
        for n, (x, y) in enumerate(((hi, hi), (hi, mid), (mid, hi), (mid, mid), (hi, low), (low, hi))):
            x_ref[BLOCK * n : BLOCK * (n + 1), :] = x
            y_ref[BLOCK * n : BLOCK * (n + 1), :] = y
        for i in range(1, BLOCKS):

            @pl.when(i > b)
            def _():
                here = slice(BLOCK * i, BLOCK * (i + 1))
                s_ref[here, pl.ds(lo, BLOCK)] = jnp.zeros((BLOCK, BLOCK), jnp.float32)
                s_ref[here, :] -= lax.dot_general(
                    x_ref[:, here], y_ref[...], (((0,), (0,)), ((), ())), preferred_element_type=jnp.float32
                )

        return carry

    lax.fori_loop(0, BLOCKS, block, 0)
    for i in range(BLOCKS):
        for j in range(BLOCKS):
            here = (slice(BLOCK * i, BLOCK * (i + 1)), slice(BLOCK * j, BLOCK * (j + 1)))
            m_ref[here] = s_ref[here] if j <= i else jnp.zeros((BLOCK, BLOCK), jnp.float32)


def gram_kernel(p_ref, o_ref):
    for i in range(BLOCKS):
        rows = lax.dot_general(
            p_ref[:, BLOCK * i : BLOCK * (i + 1)],
            p_ref[:, BLOCK * i :],
            (((0,), (0,)), ((), ())),
            precision=HIGHEST,
            preferred_element_type=jnp.float32,
        )
        for j in range(i, BLOCKS):
            o_ref[PAIRS.index((i, j))] = rows[:, BLOCK * (j - i) : BLOCK * (j - i + 1)]


def gram_blocks(projected):
    return pl.pallas_call(
        gram_kernel,
        out_shape=jax.ShapeDtypeStruct((len(PAIRS), BLOCK, BLOCK), jnp.float32),
        in_specs=[pl.BlockSpec(memory_space=pltpu.VMEM)],
        out_specs=pl.BlockSpec(memory_space=pltpu.VMEM),
        compiler_params=pltpu.CompilerParams(vmem_limit_bytes=16 * 1024 * 1024),
        cost_estimate=pl.CostEstimate(flops=2**31, bytes_accessed=2**21, transcendentals=0),
    )(projected)


def inverse_factor(core, mine, theirs):
    return pl.pallas_call(
        inverse_factor_kernel,
        out_shape=jax.ShapeDtypeStruct((RANK, RANK), jnp.float32),
        in_specs=[pl.BlockSpec(memory_space=pltpu.SMEM)] + [pl.BlockSpec(memory_space=pltpu.VMEM)] * 2,
        out_specs=pl.BlockSpec(memory_space=pltpu.VMEM),
        scratch_shapes=[
            pltpu.VMEM((RANK, RANK), jnp.float32),
            pltpu.VMEM((BLOCK, BLOCK), jnp.float32),
            pltpu.VMEM((6 * BLOCK, RANK), jnp.bfloat16),
            pltpu.VMEM((6 * BLOCK, RANK), jnp.bfloat16),
        ],
        compiler_params=pltpu.CompilerParams(vmem_limit_bytes=16 * 1024 * 1024),
        cost_estimate=pl.CostEstimate(flops=25 * 10**9, bytes_accessed=2**21, transcendentals=0),
    )(core.astype(jnp.int32).reshape(1), mine, theirs)


def weights_kernel(half_ref, b_ref, p_ref, *refs):
    *added, o_ref, w_ref = refs
    start = b_ref.shape[1] - w_ref.shape[0]
    half = half_ref[0]
    rows = b_ref[:, pl.ds(pl.multiple_of(half * start, BLOCK), w_ref.shape[0])]
    for n, piece in enumerate(pieces(p_ref[...])):
        term = lax.dot_general(rows, piece, (((0,), (0,)), ((), ())), preferred_element_type=jnp.float32)
        w_ref[...] = term if n == 0 else w_ref[...] + term
    own = w_ref[pl.ds(pl.multiple_of(half * (o_ref.shape[0] - start), SUB), o_ref.shape[0]), :]
    o_ref[...] = own + added[0][...] if added else own


def weights_half(half, blended, projected, *added):
    rows = blended.shape[1] // 2
    start = rows // BLOCK * BLOCK
    vmem = pl.BlockSpec(memory_space=pltpu.VMEM)
    return pl.pallas_call(
        weights_kernel,
        out_shape=jax.ShapeDtypeStruct((rows, RANK), jnp.float32),
        in_specs=[pl.BlockSpec(memory_space=pltpu.SMEM)] + [vmem] * (2 + len(added)),
        out_specs=vmem,
        scratch_shapes=[pltpu.VMEM((blended.shape[1] - start, RANK), jnp.float32)],
        compiler_params=pltpu.CompilerParams(vmem_limit_bytes=32 * 1024 * 1024),
        cost_estimate=pl.CostEstimate(flops=2**31, bytes_accessed=2**22, transcendentals=0),
    )(half.astype(jnp.int32).reshape(1), blended, projected, *added)


def scatter_sum(x, axis, size):
    parts = x.reshape((size, x.shape[0] // size) + x.shape[1:])
    return jnp.sum(lax.all_to_all(parts, axis, 0, 0), axis=0)


def exchange(x, axis, groups, size):
    return lax.all_to_all(jnp.broadcast_to(x, (size,) + x.shape), axis, 0, 0, axis_index_groups=groups)


def local(momentum, gradient, right_factor):
    n_col = lax.axis_size("col")
    n_row = lax.axis_size("row")
    n_z = n_row // 2
    core = lax.axis_index("row") % 2
    other = [(i, i ^ 1) for i in range(n_row)]
    along_z = [[2 * z + c for z in range(n_z)] for c in range(2)]

    def both_halves(mine):
        theirs = lax.ppermute(mine, "row", other)
        return jnp.concatenate([jnp.where(core == 0, mine, theirs), jnp.where(core == 0, theirs, mine)])

    blended = (momentum.astype(jnp.float32) + gradient.astype(jnp.float32)).astype(jnp.bfloat16)
    partial_proj = jnp.dot(blended, right_factor, preferred_element_type=jnp.float32)
    projected = exchange(scatter_sum(partial_proj, "col", n_col), "col", None, n_col).reshape(partial_proj.shape)

    theirs = weights_half(1 - core, blended, projected)
    theirs, projected = lax.optimization_barrier((theirs, projected))
    theirs = lax.ppermute(theirs, "row", other)

    packed = gram_blocks(projected).reshape(2, len(PAIRS) // 2 * BLOCK, BLOCK)
    share = packed.shape[1] // n_col
    here = lax.axis_index("col") * share
    mine, for_other = (
        lax.dynamic_slice(packed, (which, here, 0), (1, share, BLOCK))[0] for which in (core, 1 - core)
    )
    packed = mine + lax.ppermute(for_other, "row", other)

    weights = weights_half(core, blended, projected, theirs)
    weights = lax.psum_scatter(
        weights, "row", scatter_dimension=0, axis_index_groups=along_z, tiled=True
    )
    step = 1
    while step < n_z:
        packed = packed + lax.ppermute(packed, "row", [(i, i ^ (2 * step)) for i in range(n_row)])
        step *= 2
    packed = exchange(packed, "col", None, n_col).reshape(len(PAIRS) // 2, BLOCK, BLOCK)

    inverse = inverse_factor(core, packed, lax.ppermute(packed, "row", other))
    left_bf = jnp.dot(
        projected, inverse.T, precision=HIGHEST, preferred_element_type=jnp.float32
    ).astype(jnp.bfloat16)
    left_bf, weights = lax.optimization_barrier((left_bf, weights))
    back_rows = jnp.dot(weights, inverse.T, precision=HIGHEST, preferred_element_type=jnp.float32)
    half = lax.all_gather(
        back_rows.astype(jnp.bfloat16), "row", axis_index_groups=along_z, tiled=True
    )
    squares = jnp.sum(jnp.square(half.astype(jnp.float32)), axis=0).reshape(BLOCKS, BLOCK)
    squares = squares + lax.ppermute(squares, "row", other)
    squares = exchange(squares, "col", None, n_col)
    right_bf = both_halves(half)
    correction = lax.dot_general(
        left_bf, right_bf, (((1,), (1,)), ((), ())), preferred_element_type=jnp.float32
    )
    new_momentum = (blended.astype(jnp.float32) - FEEDBACK * correction).astype(jnp.bfloat16)
    squares, new_momentum = lax.optimization_barrier((squares, new_momentum))
    back_squares = jnp.sum(squares, axis=0).reshape(RANK)
    new_factor = right_bf.astype(jnp.float32) * (1.0 / jnp.sqrt(back_squares / COLS + NORM_EPS))
    factor_bf = new_factor.astype(jnp.bfloat16)
    update_full = lax.dot_general(
        left_bf, factor_bf, (((1,), (1,)), ((), ())), preferred_element_type=jnp.float32
    )
    weight_update = (update_full * math.sqrt(ROWS / RANK)).astype(jnp.bfloat16)
    return (new_momentum, weight_update, new_factor)


def solution(mesh):
    placed = (P("row", "col"), P("row", "col"), P("col", None))
    return jax.shard_map(
        local,
        mesh=mesh,
        in_specs=placed,
        out_specs=(P("row", "col"), P("row", "col"), P("col", None)),
        check_vma=False,
    )
```

```python
import math

import jax
import jax.numpy as jnp
from jax import lax
from jax.experimental import pallas as pl
from jax.experimental.pallas import tpu as pltpu
from jax.sharding import PartitionSpec as P

ROWS = 8192
COLS = 26624
RANK = 512


NORM_EPS = 1e-06
GRAM_JITTER = 0.0001
FEEDBACK = 0.25

HIGHEST = lax.Precision.HIGHEST
BLOCK = 128
BLOCKS = RANK // BLOCK
SUB = 8
GROUPS = BLOCK // SUB
PAIRS = [(i, j) for i in range(BLOCKS) for j in range(i, BLOCKS)]


def sub_row(x, k):
    return jnp.broadcast_to(x[k : k + 1, :], (SUB, BLOCK))


def lane_col(x, c):
    return jnp.broadcast_to(x[:, c : c + 1], (SUB, BLOCK))


def pieces(x):
    hi = x.astype(jnp.bfloat16)
    rest = x - hi.astype(jnp.float32)
    mid = rest.astype(jnp.bfloat16)
    return hi, mid, (rest - mid.astype(jnp.float32)).astype(jnp.bfloat16)


def stacked(*parts):
    return jnp.concatenate([x.astype(jnp.float32) for x in parts], axis=0).astype(jnp.bfloat16)


def factor_block(rows):
    sub = lax.broadcasted_iota(jnp.int32, (SUB, BLOCK), 0)
    lane = lax.broadcasted_iota(jnp.int32, (SUB, BLOCK), 1)
    out = []
    for p in range(GROUPS):
        panel = (lane >= SUB * p) & (lane < SUB * (p + 1))
        cols = [lane_col(rows[p], SUB * p + j) for j in range(SUB)]
        x = jnp.where(panel, jnp.where(lane == sub + SUB * p, 1.0, 0.0), rows[p])
        pivots, recips, row_k, upper = [], [], [], []
        for k in range(SUB):
            pivot = sub_row(cols[k], k)
            r = pl.reciprocal(pivot, approx=True)
            m = jnp.where(sub > k, cols[k] * r, 0.0)
            u = {j: sub_row(cols[j], k) for j in range(k + 1, SUB)}
            for j in range(k + 1, SUB):
                cols[j] = cols[j] - m * u[j]
            xk = sub_row(x, k)
            if k < SUB - 1:
                x = x - m * xk
            pivots.append(pivot)
            recips.append(r)
            row_k.append(xk)
            upper.append(u)
        d8 = pivots[0]
        for k in range(1, SUB):
            d8 = jnp.where(sub == k, pivots[k], d8)
        out.append(jnp.where(lane < SUB * (p + 1), x * lax.rsqrt(d8), 0.0))
        if p + 1 < GROUPS:
            b = [lane_col(rows[p + 1], SUB * p + j) for j in range(SUB)]
            y = jnp.where(panel, 0.0, rows[p + 1])
            for k in range(SUB):
                m = b[k] * recips[k]
                for j in range(k + 1, SUB):
                    b[j] = b[j] - m * upper[k][j]
                y = y - m * row_k[k]
            rows[p + 1] = y
        if p + 2 < GROUPS:
            r8 = recips[0]
            for k in range(1, SUB):
                r8 = jnp.where(sub == k, recips[k], r8)
            hi, mid, low = pieces(x)
            hi2, mid2, low2 = pieces(x * r8)
            product = lax.dot_general(
                stacked(hi, hi, mid, mid, hi, low),
                stacked(hi2, mid2, hi2, mid2, low2, hi2),
                (((0,), (0,)), ((), ())),
                preferred_element_type=jnp.float32,
            )
            for q in range(p + 2, GROUPS):
                rows[q] = jnp.where(panel, 0.0, rows[q]) - product[SUB * q : SUB * (q + 1), :]
    return out


def inverse_factor_kernel(core_ref, mine_ref, theirs_ref, m_ref, s_ref, d_ref, x_ref, y_ref):
    half = mine_ref.shape[0]

    def gram(n):
        return jnp.where(core_ref[0] == n // half, mine_ref[n % half], theirs_ref[n % half])

    eye = (
        lax.broadcasted_iota(jnp.int32, (BLOCK, BLOCK), 0)
        == lax.broadcasted_iota(jnp.int32, (BLOCK, BLOCK), 1)
    )
    diagonal = jnp.zeros((BLOCK, BLOCK), jnp.float32)
    for n, (i, j) in enumerate(PAIRS):
        if i == j:
            diagonal += jnp.where(eye, gram(n), 0.0)
    jitter = (GRAM_JITTER / RANK) * jnp.sum(diagonal)
    s_ref[...] = jnp.zeros_like(s_ref)
    for n, (i, j) in enumerate(PAIRS):
        x = gram(n)
        if i == j:
            x = x + jnp.where(eye, jitter, 0.0)
        s_ref[BLOCK * i : BLOCK * (i + 1), BLOCK * j : BLOCK * (j + 1)] = x

    def block(b, carry):
        lo = pl.multiple_of(b * BLOCK, BLOCK)
        rows = [s_ref[pl.ds(lo + SUB * q, SUB), pl.ds(lo, BLOCK)] for q in range(GROUPS)]
        for q, x in enumerate(factor_block(rows)):
            d_ref[SUB * q : SUB * (q + 1), :] = x
        m_bb = d_ref[...]
        hi, mid, low = pieces(m_bb)
        first = jnp.concatenate([hi, hi, mid, mid, hi, low], axis=1)
        hi, mid, low = pieces(s_ref[pl.ds(lo, BLOCK), :])
        second = jnp.concatenate([hi, mid, hi, mid, low, hi], axis=0)
        s_ref[pl.ds(lo, BLOCK), :] = jnp.dot(first, second, preferred_element_type=jnp.float32)
        s_ref[pl.ds(lo, BLOCK), pl.ds(lo, BLOCK)] = m_bb
        hi, mid, low = pieces(s_ref[pl.ds(lo, BLOCK), :])
        for n, (x, y) in enumerate(((hi, hi), (hi, mid), (mid, hi), (mid, mid), (hi, low), (low, hi))):
            x_ref[BLOCK * n : BLOCK * (n + 1), :] = x
            y_ref[BLOCK * n : BLOCK * (n + 1), :] = y
        for i in range(1, BLOCKS):

            @pl.when(i > b)
            def _():
                here = slice(BLOCK * i, BLOCK * (i + 1))
                s_ref[here, pl.ds(lo, BLOCK)] = jnp.zeros((BLOCK, BLOCK), jnp.float32)
                s_ref[here, :] -= lax.dot_general(
                    x_ref[:, here], y_ref[...], (((0,), (0,)), ((), ())), preferred_element_type=jnp.float32
                )

        return carry

    lax.fori_loop(0, BLOCKS, block, 0)
    for i in range(BLOCKS):
        for j in range(BLOCKS):
            here = (slice(BLOCK * i, BLOCK * (i + 1)), slice(BLOCK * j, BLOCK * (j + 1)))
            m_ref[here] = s_ref[here] if j <= i else jnp.zeros((BLOCK, BLOCK), jnp.float32)


def gram_kernel(p_ref, o_ref):
    for i in range(BLOCKS):
        rows = lax.dot_general(
            p_ref[:, BLOCK * i : BLOCK * (i + 1)],
            p_ref[:, BLOCK * i :],
            (((0,), (0,)), ((), ())),
            precision=HIGHEST,
            preferred_element_type=jnp.float32,
        )
        for j in range(i, BLOCKS):
            o_ref[PAIRS.index((i, j))] = rows[:, BLOCK * (j - i) : BLOCK * (j - i + 1)]


def gram_blocks(projected):
    return pl.pallas_call(
        gram_kernel,
        out_shape=jax.ShapeDtypeStruct((len(PAIRS), BLOCK, BLOCK), jnp.float32),
        in_specs=[pl.BlockSpec(memory_space=pltpu.VMEM)],
        out_specs=pl.BlockSpec(memory_space=pltpu.VMEM),
        compiler_params=pltpu.CompilerParams(vmem_limit_bytes=14 * 1024 * 1024),
        cost_estimate=pl.CostEstimate(flops=2**31, bytes_accessed=2**21, transcendentals=0),
    )(projected)


def inverse_factor(core, mine, theirs):
    return pl.pallas_call(
        inverse_factor_kernel,
        out_shape=jax.ShapeDtypeStruct((RANK, RANK), jnp.float32),
        in_specs=[pl.BlockSpec(memory_space=pltpu.SMEM)] + [pl.BlockSpec(memory_space=pltpu.VMEM)] * 2,
        out_specs=pl.BlockSpec(memory_space=pltpu.VMEM),
        scratch_shapes=[
            pltpu.VMEM((RANK, RANK), jnp.float32),
            pltpu.VMEM((BLOCK, BLOCK), jnp.float32),
            pltpu.VMEM((6 * BLOCK, RANK), jnp.bfloat16),
            pltpu.VMEM((6 * BLOCK, RANK), jnp.bfloat16),
        ],
        compiler_params=pltpu.CompilerParams(vmem_limit_bytes=14 * 1024 * 1024),
        cost_estimate=pl.CostEstimate(flops=25 * 10**9, bytes_accessed=2**21, transcendentals=0),
    )(core.astype(jnp.int32).reshape(1), mine, theirs)


def weights_kernel(half_ref, b_ref, p_ref, *refs):
    *added, o_ref, w_ref = refs
    start = b_ref.shape[1] - w_ref.shape[0]
    half = half_ref[0]
    rows = b_ref[:, pl.ds(pl.multiple_of(half * start, BLOCK), w_ref.shape[0])]
    for n, piece in enumerate(pieces(p_ref[...])):
        term = lax.dot_general(rows, piece, (((0,), (0,)), ((), ())), preferred_element_type=jnp.float32)
        w_ref[...] = term if n == 0 else w_ref[...] + term
    own = w_ref[pl.ds(pl.multiple_of(half * (o_ref.shape[0] - start), SUB), o_ref.shape[0]), :]
    o_ref[...] = own + added[0][...] if added else own


def weights_half(half, blended, projected, *added):
    rows = blended.shape[1] // 2
    start = rows // BLOCK * BLOCK
    vmem = pl.BlockSpec(memory_space=pltpu.VMEM)
    return pl.pallas_call(
        weights_kernel,
        out_shape=jax.ShapeDtypeStruct((rows, RANK), jnp.float32),
        in_specs=[pl.BlockSpec(memory_space=pltpu.SMEM)] + [vmem] * (2 + len(added)),
        out_specs=vmem,
        scratch_shapes=[pltpu.VMEM((blended.shape[1] - start, RANK), jnp.float32)],
        compiler_params=pltpu.CompilerParams(vmem_limit_bytes=14 * 1024 * 1024),
        cost_estimate=pl.CostEstimate(flops=2**31, bytes_accessed=2**22, transcendentals=0),
    )(half.astype(jnp.int32).reshape(1), blended, projected, *added)


def scatter_sum(x, axis, size):
    parts = x.reshape((size, x.shape[0] // size) + x.shape[1:])
    return jnp.sum(lax.all_to_all(parts, axis, 0, 0), axis=0)


def exchange(x, axis, groups, size):
    return lax.all_to_all(jnp.broadcast_to(x, (size,) + x.shape), axis, 0, 0, axis_index_groups=groups)


def local(momentum, gradient, right_factor):
    n_col = lax.axis_size("col")
    n_row = lax.axis_size("row")
    n_z = n_row // 2
    core = lax.axis_index("row") % 2
    other = [(i, i ^ 1) for i in range(n_row)]
    along_z = [[2 * z + c for z in range(n_z)] for c in range(2)]

    def both_halves(mine):
        theirs = lax.ppermute(mine, "row", other)
        return jnp.concatenate([jnp.where(core == 0, mine, theirs), jnp.where(core == 0, theirs, mine)])

    blended = (momentum.astype(jnp.float32) + gradient.astype(jnp.float32)).astype(jnp.bfloat16)
    partial_proj = jnp.dot(blended, right_factor, preferred_element_type=jnp.float32)
    projected = exchange(scatter_sum(partial_proj, "col", n_col), "col", None, n_col).reshape(partial_proj.shape)

    theirs = weights_half(1 - core, blended, projected)
    theirs, projected = lax.optimization_barrier((theirs, projected))
    theirs = lax.ppermute(theirs, "row", other)

    packed = gram_blocks(projected).reshape(2, len(PAIRS) // 2 * BLOCK, BLOCK)
    share = packed.shape[1] // n_col
    here = lax.axis_index("col") * share
    mine, for_other = (
        lax.dynamic_slice(packed, (which, here, 0), (1, share, BLOCK))[0] for which in (core, 1 - core)
    )
    packed = mine + lax.ppermute(for_other, "row", other)

    weights = weights_half(core, blended, projected, theirs)
    weights = lax.psum_scatter(
        weights, "row", scatter_dimension=0, axis_index_groups=along_z, tiled=True
    )
    packed = jnp.sum(exchange(packed, "row", along_z, n_z), axis=0)
    packed = exchange(packed, "col", None, n_col).reshape(len(PAIRS) // 2, BLOCK, BLOCK)

    inverse = inverse_factor(core, packed, lax.ppermute(packed, "row", other))
    left_bf = jnp.dot(
        projected, inverse.T, precision=HIGHEST, preferred_element_type=jnp.float32
    ).astype(jnp.bfloat16)
    left_bf, weights = lax.optimization_barrier((left_bf, weights))
    back_rows = jnp.dot(weights, inverse.T, precision=HIGHEST, preferred_element_type=jnp.float32)
    half = lax.all_gather(
        back_rows.astype(jnp.bfloat16), "row", axis_index_groups=along_z, tiled=True
    )
    squares = jnp.sum(jnp.square(half.astype(jnp.float32)), axis=0).reshape(BLOCKS, BLOCK)
    squares = squares + lax.ppermute(squares, "row", other)
    squares = exchange(squares, "col", None, n_col)
    right_bf = both_halves(half)
    correction = lax.dot_general(
        left_bf, right_bf, (((1,), (1,)), ((), ())), preferred_element_type=jnp.float32
    )
    new_momentum = (blended.astype(jnp.float32) - FEEDBACK * correction).astype(jnp.bfloat16)
    squares, new_momentum = lax.optimization_barrier((squares, new_momentum))
    back_squares = jnp.sum(squares, axis=0).reshape(RANK)
    new_factor = right_bf.astype(jnp.float32) * (1.0 / jnp.sqrt(back_squares / COLS + NORM_EPS))
    factor_bf = new_factor.astype(jnp.bfloat16)
    update_full = lax.dot_general(
        left_bf, factor_bf, (((1,), (1,)), ((), ())), preferred_element_type=jnp.float32
    )
    weight_update = (update_full * math.sqrt(ROWS / RANK)).astype(jnp.bfloat16)
    return (new_momentum, weight_update, new_factor)


def solution(mesh):
    placed = (P("row", "col"), P("row", "col"), P("col", None))
    return jax.shard_map(
        local,
        mesh=mesh,
        in_specs=placed,
        out_specs=(P("row", "col"), P("row", "col"), P("col", None)),
        check_vma=False,
    )
```
